128 devices in a mesh: grp: 8 (over z, core), dev: 16 (over x, y).
Axes of the slice: x: 4, y: 4, z: 4, core: 2. Of those that a mesh axis runs over, the one named last changes fastest.
Arguments:
- velocity_old: float32 [512, 3, 32, 1024], P(('grp', 'dev')), may hold values from -6 to 6
- viscosity_old: float32 [512, 32, 1024], P(('grp', 'dev')), may hold values from 0.25 to 4
- source: int32 [512], replicated, may hold values from 0 to 511, as said below
Outputs:
- velocity_new: float32 [512, 3, 32, 1024], P(('grp', 'dev'))
The draws below stay inside these ranges and needn't reach their ends.
Inputs may be any that keep to these rules, and one draw needn't show every extreme that they name: `source`: A permutation; the old block of new block b lies in the same agglomeration group and has the same place among its device's 4 blocks; the 4 blocks of a new device come from 4 different old devices of its group, and each old device sends 1 block to each of 4 different new devices.
All inputs are finite; a program needn't handle non-finite values.
Results may differ from the reference program's by a relative error of at most 0.0001.
Values sent between devices are 32-bit elements; how exact they have to be, the bound alone decides.
A program may use at most 256 MiB of HBM per device.

```python
import math
import jax
import jax.numpy as jnp

SIDE = 32
BLK_DEV = 4
SWEEPS = 2
BOTTOM = 8
BLOCKS = 512
N_GRP = 8
N_DEV = 16


def draw_source(key, part):

    def one_group(group_no):
        group_key = jax.random.fold_in(key, group_no)
        order = jax.random.permutation(jax.random.fold_in(group_key, 1), N_DEV)
        steps = jax.random.permutation(jax.random.fold_in(group_key, 2), N_DEV - 1)[:BLK_DEV - 1] + 1
        offsets = jnp.concatenate([jnp.zeros((1,), jnp.int32), steps.astype(jnp.int32)])
        member_ids = jnp.arange(N_DEV, dtype=jnp.int32)
        owners = order[(member_ids[:, None] + offsets[None, :]) % N_DEV]
        return ((group_no * N_DEV + owners) * BLK_DEV + jnp.arange(BLK_DEV, dtype=jnp.int32)[None, :]).astype(jnp.int32)
    return jax.vmap(one_group)(jnp.arange(N_GRP, dtype=jnp.int32)).reshape(BLOCKS).astype(jnp.int32)


def block_scale(stream_key, shape, shards, low, largest):
    level, own = 1.0, jax.random.fold_in(stream_key, 6)
    for axis_at, shards_of in shards:
        steps = jnp.exp(jax.random.uniform(jax.random.fold_in(own, axis_at), (shards_of,), jnp.float32, low / len(shards), largest / len(shards)))
        level = level * jnp.repeat(steps, shape[axis_at] // shards_of).reshape([-1 if axis == axis_at else 1 for axis in range(len(shape))])
    return level


def bell_draw(own_key, shape, width, bound, shards=(), held_as=jnp.bfloat16):
    level = block_scale(own_key, shape, shards, -0.22, 0.18) if shards else 1.0
    values = jax.random.normal(own_key, shape, jnp.float32) * width * level
    return jnp.minimum(jnp.maximum(values, -bound), bound).astype(held_as)


def setup_inputs(seed: int = 0) -> dict:
    splits = jax.random.split(jax.random.key(seed), 4)
    return {
        "velocity_old": bell_draw(splits[0], (BLOCKS, 3, SIDE, SIDE * SIDE), 1.0, 6.0, ((0, 128),), jnp.float32),
        "viscosity_old": jnp.clip(jnp.exp(math.log(4.0) - 2.7725887 * jax.random.uniform(splits[1], (BLOCKS, SIDE, SIDE * SIDE), jnp.float32) ** block_scale(splits[1], (BLOCKS, SIDE, SIDE * SIDE), ((0, 128),), -0.2, 0.2)), 0.25, 4.0),
        "source": draw_source(jax.random.fold_in(splits[3], 71), 0),
    }


RELAX_WEIGHT = 0.8
DIFFUSION_NUMBER = 1000.0

def blocks_to_grid(blocks):
    num_blocks, channels, edge_len = (blocks.shape[0], blocks.shape[1], blocks.shape[2])
    columns = num_blocks // 4
    parted = blocks.reshape(columns, 2, 2, channels, edge_len, edge_len, edge_len)
    parted = parted.transpose(3, 0, 6, 1, 4, 2, 5)
    return parted.reshape(channels, columns * edge_len, 4 * edge_len * edge_len)

def grid_to_blocks(grid):
    channels, length, plane = grid.shape
    edge_len = math.isqrt(plane) // 2
    columns = length // edge_len
    parted = grid.reshape(channels, columns, edge_len, 2, edge_len, 2, edge_len)
    parted = parted.transpose(1, 3, 5, 0, 4, 6, 2)
    return parted.reshape(columns * 4, channels, edge_len, edge_len * edge_len)

def flat_neighbors(array):
    plane = array.shape[2]
    width_y = math.isqrt(plane)
    middle = array[:, 1:-1]
    padded = jnp.pad(middle, ((0, 0), (0, 0), (width_y, width_y)))
    column = jnp.arange(plane) % width_y
    lower_y = jnp.where(column == 0, 0.0, padded[:, :, width_y - 1:width_y - 1 + plane])
    upper_y = jnp.where(column == width_y - 1, 0.0, padded[:, :, width_y + 1:width_y + 1 + plane])
    return (middle, (array[:, :-2], array[:, 2:], padded[:, :, 0:plane], padded[:, :, 2 * width_y:2 * width_y + plane], lower_y, upper_y))

def coefficients(viscous, level_coef, pad_along):
    middle, beside_all = flat_neighbors(pad_along(viscous))
    face_coef = tuple((0.5 * (middle + neighbor) for neighbor in beside_all))
    summed = face_coef[0] + face_coef[1] + face_coef[2] + face_coef[3] + face_coef[4] + face_coef[5]
    diagonal = 1.0 + level_coef * summed
    return (face_coef, diagonal)

def operate(solution, face_coef, diagonal, level_coef, pad_along):
    middle, beside_all = flat_neighbors(pad_along(solution))
    summed = face_coef[0] * beside_all[0]
    for index_no in range(1, 6):
        summed = summed + face_coef[index_no] * beside_all[index_no]
    return diagonal * solution - level_coef * summed

def smooth(solution, right_side, face_coef, diagonal, level_coef, pad_along, repeats):
    for sweep_no in range(repeats):
        solution = solution + RELAX_WEIGHT * (right_side - operate(solution, face_coef, diagonal, level_coef, pad_along)) / diagonal
    return solution

def coarsen(grid):
    channels, length, plane = grid.shape
    width_y = math.isqrt(plane)
    shaped = grid.reshape(channels, length // 2, 2, width_y // 2, 2, width_y // 2, 2)
    return shaped.mean(axis=(2, 4, 6)).reshape(channels, length // 2, plane // 4)

def refine(grid):
    channels, length, plane = grid.shape
    width_y = math.isqrt(plane)
    shaped = grid.reshape(channels, length, 1, width_y, 1, width_y, 1)
    shaped = jnp.broadcast_to(shaped, (channels, length, 2, width_y, 2, width_y, 2))
    return shaped.reshape(channels, 2 * length, 4 * plane)

def vcycle_solve(right_side, viscous, pad_along, bottom_solve):
    stored = []
    solution = right_side
    level_rhs = right_side
    for level_no in range(3):
        level_coef = DIFFUSION_NUMBER / 4.0 ** level_no
        face_coef, diagonal = coefficients(viscous, level_coef, pad_along)
        solution = smooth(solution, level_rhs, face_coef, diagonal, level_coef, pad_along, SWEEPS)
        residue = level_rhs - operate(solution, face_coef, diagonal, level_coef, pad_along)
        stored.append((solution, level_rhs, face_coef, diagonal, level_coef))
        level_rhs = coarsen(residue)
        viscous = coarsen(viscous)
        solution = jnp.zeros_like(level_rhs)
    solution = bottom_solve(level_rhs, viscous)
    for level_no in (2, 1, 0):
        before, level_rhs, face_coef, diagonal, level_coef = stored[level_no]
        solution = smooth(before + refine(solution), level_rhs, face_coef, diagonal, level_coef, pad_along, SWEEPS)
    return solution

def stream_pad(array):
    return jnp.pad(array, ((0, 0), (1, 1), (0, 0)))

def global_bottom(level_rhs, viscous):
    level_coef = DIFFUSION_NUMBER / 64.0
    face_coef, diagonal = coefficients(viscous, level_coef, stream_pad)
    return smooth(jnp.zeros_like(level_rhs), level_rhs, face_coef, diagonal, level_coef, stream_pad, BOTTOM)

def reference(velocity_old, viscosity_old, source):
    velocity = jnp.take(velocity_old, source, axis=0)
    viscous_new = jnp.take(viscosity_old, source, axis=0)
    right_side = blocks_to_grid(velocity)
    viscous = blocks_to_grid(viscous_new[:, None])
    solution = vcycle_solve(right_side, viscous, stream_pad, global_bottom)
    return grid_to_blocks(solution)
```

```python
import jax
import jax.numpy as jnp
from jax import lax
from jax.experimental import pallas as pl
from jax.experimental.pallas import tpu as pltpu
from jax.sharding import PartitionSpec as P

F32 = jnp.float32
SIDE = 32
LANES = 128
DIFFUSION_NUMBER = 1000.0
RELAX = 0.8
BOTTOM = 8
LANE_SLOTS = (0, 2, 1, 3)
H0, H1, H2 = 4, 5, 6
N0, N1, N2, N3 = 32, 16, 8, 4
REACH = 3
H3 = REACH * N3
VMEM_LIMIT = 48 * 1024 * 1024
MESH = pl.DeviceIdType.MESH
HIGHEST = lax.Precision.HIGHEST


def positions():
    grp, dev = lax.axis_index("grp"), lax.axis_index("dev")
    n_grp, n_dev = lax.axis_size("grp"), lax.axis_size("dev")
    return grp, dev, n_grp, n_dev


def stream_device(offset):
    grp, dev, n_grp, n_dev = positions()
    at = lax.rem(grp * n_dev + dev + offset + n_grp * n_dev, n_grp * n_dev)
    return (at // n_dev, lax.rem(at, n_dev))


def multiple(value, of):
    return pl.multiple_of(value, of)


def regrid_kernel(
    source_ref, vel_ref, vis_ref, o_nu, o_0, o_1, o_2,
    st_0, st_1, st_2, st_3, mid_0, mid_1, mid_2, mid_3, as_0, as_1, as_2, as_3,
    send_1, recv_1, send_2, recv_2, send_h, recv_h,
):
    grp, dev, n_grp, n_dev = positions()
    each = SIDE // n_dev
    rows = each * SIDE
    outs = (o_nu, o_0, o_1, o_2)
    stages = (st_0, st_1, st_2, st_3)
    mids = (mid_0, mid_1, mid_2, mid_3)
    asms = (as_0, as_1, as_2, as_3)
    left, right = stream_device(-1), stream_device(1)

    barrier = pltpu.get_barrier_semaphore()

    def greet(t, carry):
        pl.semaphore_signal(
            barrier, inc=1, device_id=(grp, lax.rem(dev + t, n_dev)), device_id_type=MESH
        )
        return carry

    lax.fori_loop(1, n_dev, greet, 0)
    for beside in (left, right):
        pl.semaphore_signal(barrier, inc=1, device_id=beside, device_id_type=MESH)

    def transpose_field(f):
        def tile(t, carry):
            lanes = pl.ds(multiple(t * LANES, LANES), LANES)
            if f == 0:
                parts = [vis_ref[b, :, lanes] for b in LANE_SLOTS]
            else:
                parts = [vel_ref[b, f - 1, :, lanes] for b in LANE_SLOTS]
            turned = jnp.concatenate(parts, axis=0).T
            for jj in range(4):
                stages[f][pl.ds(4 * t + jj, SIDE, stride=SIDE), :] = turned[
                    SIDE * jj : SIDE * jj + SIDE
                ]
            return carry

        lax.fori_loop(0, 8, tile, 0)

    def spread(f):
        def send(t, carry):
            to = lax.rem(dev + t, n_dev)
            pltpu.make_async_remote_copy(
                src_ref=stages[f].at[pl.ds(multiple(to * rows, rows), rows)],
                dst_ref=mids[f].at[dev],
                send_sem=send_1.at[f],
                recv_sem=recv_1.at[f],
                device_id=(grp, to),
                device_id_type=MESH,
            ).start()
            return carry

        pltpu.make_async_copy(
            stages[f].at[pl.ds(multiple(dev * rows, rows), rows)], mids[f].at[dev], recv_1.at[f]
        ).start()
        lax.fori_loop(1, n_dev, send, 0)

    group_of_lane = lax.broadcasted_iota(jnp.int32, (rows, LANES), 1) // SIDE

    def collect(f):
        pltpu.make_async_copy(mids[f], mids[f], recv_1.at[f]).wait()

        def assemble(to):
            base = (grp * n_dev + to) * 4
            made = None
            for at, slot in enumerate(LANE_SLOTS):
                old = lax.rem(source_ref[base + slot] // 4, n_dev)
                piece = mids[f][old]
                made = piece if made is None else jnp.where(group_of_lane == at, piece, made)
            asms[f][to] = made.reshape(each, SIDE, LANES)

        def send(t, carry):
            to = lax.rem(dev + t, n_dev)
            assemble(to)
            pltpu.make_async_remote_copy(
                src_ref=asms[f].at[to],
                dst_ref=outs[f].at[pl.ds(H0 + dev * each, each)],
                send_sem=send_2.at[f],
                recv_sem=recv_2.at[f],
                device_id=(grp, to),
                device_id_type=MESH,
            ).start()
            return carry

        assemble(dev)
        pltpu.make_async_copy(
            asms[f].at[dev], outs[f].at[pl.ds(H0 + dev * each, each)], recv_2.at[f]
        ).start()
        lax.fori_loop(1, n_dev, send, 0)

    def halo_copy(f, side):
        src = outs[f].at[pl.ds(H0 if side == 0 else N0, H0)]
        dst = outs[f].at[pl.ds(H0 + N0 if side == 0 else 0, H0)]
        return pltpu.make_async_remote_copy(
            src_ref=src,
            dst_ref=dst,
            send_sem=send_h.at[f, side],
            recv_sem=recv_h.at[f, side],
            device_id=left if side == 0 else right,
            device_id_type=MESH,
        )

    transpose_field(0)
    pl.semaphore_wait(barrier, n_dev + 1)
    spread(0)
    for f in range(1, 4):
        transpose_field(f)
        spread(f)
    for f in range(4):
        collect(f)
    for f in range(4):
        own = outs[f].at[pl.ds(H0, N0)]
        pltpu.make_async_copy(own, own, recv_2.at[f]).wait()
        for side in (0, 1):
            halo_copy(f, side).start()
    at = grp * n_dev + dev
    for f in range(4):
        for side in (0, 1):
            halo_copy(f, side).wait()

        @pl.when(at == 0)
        def _():
            outs[f][pl.ds(0, H0)] = jnp.zeros((H0, SIDE, LANES), F32)

        @pl.when(at == n_grp * n_dev - 1)
        def _():
            outs[f][pl.ds(H0 + N0, H0)] = jnp.zeros((H0, SIDE, LANES), F32)

    for f in range(4):
        most = stages[f].at[pl.ds(0, (n_dev - 1) * rows)]
        pltpu.make_async_copy(most, most, send_1.at[f]).wait()
        most = asms[f].at[pl.ds(0, n_dev - 1)]
        pltpu.make_async_copy(most, most, send_2.at[f]).wait()


def regrid(n_dev, source, velocity_old, viscosity_old):
    each = SIDE // n_dev
    vmem = pl.BlockSpec(memory_space=pltpu.VMEM)
    extended = jax.ShapeDtypeStruct((N0 + 2 * H0, SIDE, LANES), F32)
    return pl.pallas_call(
        regrid_kernel,
        out_shape=[extended] * 4,
        in_specs=[pl.BlockSpec(memory_space=pltpu.SMEM), vmem, vmem],
        out_specs=[vmem] * 4,
        scratch_shapes=[pltpu.VMEM((SIDE * SIDE, LANES), F32)] * 4
        + [pltpu.VMEM((n_dev, each * SIDE, LANES), F32)] * 4
        + [pltpu.VMEM((n_dev, each, SIDE, LANES), F32)] * 4
        + [pltpu.SemaphoreType.DMA((4,))] * 4
        + [pltpu.SemaphoreType.DMA((4, 2))] * 2,
        compiler_params=pltpu.CompilerParams(
            collective_id=0, has_side_effects=True, vmem_limit_bytes=VMEM_LIMIT
        ),
        name="regrid",
    )(source, velocity_old, viscosity_old)


class Level:
    def __init__(self, rows, wide, d):
        self.rows, self.wide, self.d = rows, wide, d
        self.shape = (rows, LANES)
        row = lax.broadcasted_iota(jnp.int32, self.shape, 0)
        lane = lax.broadcasted_iota(jnp.int32, self.shape, 1)
        deep = lax.rem(lane, wide)
        far = LANES - wide
        self.ok_zm = deep >= d
        self.ok_zp = deep < wide - d
        self.ok_ym = (row >= d) | (lane >= wide)
        self.ok_yp = (row < rows - d) | (lane < far)
        edge = lax.broadcasted_iota(jnp.int32, (8, LANES), 0)
        self.edge_m = edge < d
        self.edge_p = edge >= 8 - d

    def beside(self, a):
        rows, wide, d = self.rows, self.wide, self.d
        zm = pltpu.roll(a, d, 1)
        zp = pltpu.roll(a, LANES - d, 1)
        ym = pltpu.roll(a, d, 0)
        yp = pltpu.roll(a, rows - d, 0)
        head = ym[:8]
        head = jnp.where(self.edge_m, pltpu.roll(head, wide, 1), head)
        tail = yp[rows - 8 :]
        tail = jnp.where(self.edge_p, pltpu.roll(tail, LANES - wide, 1), tail)
        if rows > 8:
            ym = jnp.concatenate([head, ym[8:]], axis=0)
            yp = jnp.concatenate([yp[: rows - 8], tail], axis=0)
        else:
            ym, yp = head, tail
        return zm, zp, ym, yp


def pair_sum(a, d):
    row = lax.broadcasted_iota(jnp.int32, a.shape, 0)
    lane = lax.broadcasted_iota(jnp.int32, a.shape, 1)
    first = lax.rem(row // d, 2) == 0
    a = a + jnp.where(first, pltpu.roll(a, a.shape[0] - d, 0), pltpu.roll(a, d, 0))
    first = lax.rem(lane // d, 2) == 0
    return a + jnp.where(first, pltpu.roll(a, LANES - d, 1), pltpu.roll(a, d, 1))


def weights(level, coef, lo, hi, nu_at, rhs_at, inside, g_ref, iw_ref, s_refs, also=None):
    def plane(n, carry):
        nu = nu_at(n)
        xm, xp = nu_at(n - 1), nu_at(n + 1)
        zm, zp, ym, yp = level.beside(nu)
        zm = jnp.where(level.ok_zm, zm, 0.0)
        zp = jnp.where(level.ok_zp, zp, 0.0)
        ym = jnp.where(level.ok_ym, ym, 0.0)
        yp = jnp.where(level.ok_yp, yp, 0.0)
        total = 6.0 * nu + ((xm + xp) + (zm + zp) + (ym + yp))
        diag = 1.0 + (0.5 * coef) * total
        w = RELAX / diag
        k = w * jnp.where(inside(n), 0.5 * coef, 0.0)
        g_ref[0, n] = k * (nu + xm)
        g_ref[1, n] = k * (nu + xp)
        g_ref[2, n] = jnp.where(level.ok_zm, k * (nu + zm), 0.0)
        g_ref[3, n] = jnp.where(level.ok_zp, k * (nu + zp), 0.0)
        g_ref[4, n] = jnp.where(level.ok_ym, k * (nu + ym), 0.0)
        g_ref[5, n] = jnp.where(level.ok_yp, k * (nu + yp), 0.0)
        iw_ref[n] = diag * (1.0 / RELAX)
        for c in range(3):
            s_refs[c][n] = w * rhs_at(c, n)
        return carry

    lax.fori_loop(lo, hi, plane, 0)


def gathered(level, g, src, n):
    zm, zp, ym, yp = level.beside(src[n])
    return (
        (g[0] * src[n - 1] + g[1] * src[n + 1])
        + (g[2] * zm + g[3] * zp)
        + (g[4] * ym + g[5] * yp)
    )


def sweep(level, lo, hi, g_ref, s_refs, srcs, dsts, shift=0):
    def plane(n, carry):
        g = [g_ref[i, n] for i in range(6)]
        for c in range(3):
            dsts[c][n - shift] = (1.0 - RELAX) * srcs[c][n] + (
                s_refs[c][n] + gathered(level, g, srcs[c], n)
            )
        return carry

    lax.fori_loop(lo, hi, plane, 0)


def residual(level, n, g_ref, iw_ref, s_refs, srcs):
    g = [g_ref[i, n] for i in range(6)]
    return [
        iw_ref[n] * ((s_refs[c][n] + gathered(level, g, srcs[c], n)) - RELAX * srcs[c][n])
        for c in range(3)
    ]


def vcycle_kernel(
    nu_0, r_0, r_1, r_2, o_0, o_1, o_2,
    g0, iw0, s0_0, s0_1, s0_2, a0_0, a0_1, a0_2, b0_0, b0_1, b0_2, tmp, half,
    x1, g1, iw1, s1_0, s1_1, s1_2, a1_0, a1_1, a1_2,
    x2, g2, iw2, s2_0, s2_1, s2_2, a2_0, a2_1, a2_2,
    x3, g3, iw3, s3_0, s3_1, s3_2, a3_0, a3_1, a3_2,
    pk2, pk3, send_1, recv_1, send_2, recv_2, send_3, recv_3,
):
    grp, dev, n_grp, n_dev = positions()
    at = grp * n_dev + dev
    count = n_grp * n_dev
    hops = [k for k in range(-REACH, REACH + 1) if k]

    barrier = pltpu.get_barrier_semaphore()
    for k in hops:
        pl.semaphore_signal(barrier, inc=1, device_id=stream_device(k), device_id_type=MESH)

    def inside_of(own, halo):
        def inside(n):
            cell = at * own + n - halo
            return (cell >= 0) & (cell < count * own)

        return inside

    in0, in1 = inside_of(N0, H0), inside_of(N1, H1)
    in2, in3 = inside_of(N2, H2), inside_of(N3, H3)
    rhs0 = (r_0, r_1, r_2)
    s0, a0, b0 = (s0_0, s0_1, s0_2), (a0_0, a0_1, a0_2), (b0_0, b0_1, b0_2)
    s1, a1 = (s1_0, s1_1, s1_2), (a1_0, a1_1, a1_2)
    s2, a2 = (s2_0, s2_1, s2_2), (a2_0, a2_1, a2_2)
    s3, a3 = (s3_0, s3_1, s3_2), (a3_0, a3_1, a3_2)

    fine = Level(SIDE, 2 * SIDE, 1)
    lane_f = lax.broadcasted_iota(jnp.int32, (LANES, LANES), 0)
    lane_c = lax.broadcasted_iota(jnp.int32, (LANES, LANES), 1)
    target = (lane_f // 64) * 64 + lax.rem(lane_f, 64) // 2
    down_m = [jnp.where(lane_c == target + 32 * jh, 0.5, 0.0).astype(F32) for jh in (0, 1)]
    target_t = (lane_c // 64) * 64 + lax.rem(lane_c, 64) // 2
    up_m = [jnp.where(lane_f == target_t + 32 * jh, 1.0, 0.0).astype(F32) for jh in (0, 1)]

    def rows_halved(f, m, total):
        tmp[f] = total
        pairs = 0.25 * (tmp[f, pl.ds(0, 16, stride=2), :] + tmp[f, pl.ds(1, 16, stride=2), :])
        half[f, 0, m] = pairs[:8]
        half[f, 1, m] = pairs[8:]

    def lanes_halved(f):
        made = None
        for jh in (0, 1):
            part = jnp.dot(
                half[f, jh, :N1].reshape(N1 * 8, LANES), down_m[jh],
                precision=HIGHEST, preferred_element_type=F32,
            )
            made = part if made is None else made + part
        x1[pl.ds(H1, N1), f] = made.reshape(N1, 8, LANES)

    weights(
        fine, DIFFUSION_NUMBER, 1, N0 + 2 * H0 - 1, lambda n: nu_0[n], lambda c, n: rhs0[c][n],
        in0, g0, iw0, s0,
    )

    def nu_pairs(m, carry):
        rows_halved(3, m, nu_0[H0 + 2 * m] + nu_0[H0 + 2 * m + 1])
        return carry

    lax.fori_loop(0, N1, nu_pairs, 0)
    lanes_halved(3)
    sweep(fine, 1, N0 + 2 * H0 - 1, g0, s0, rhs0, a0)
    sweep(fine, 2, N0 + 2 * H0 - 2, g0, s0, a0, b0)

    def down_0(m, carry):
        n = H0 + 2 * m
        first = residual(fine, n, g0, iw0, s0, b0)
        second = residual(fine, n + 1, g0, iw0, s0, b0)
        for c in range(3):
            rows_halved(c, m, first[c] + second[c])
        return carry

    lax.fori_loop(0, N1, down_0, 0)
    for c in range(3):
        lanes_halved(c)

    pl.semaphore_wait(barrier, len(hops))

    def exchange(k, src, dst, send, recv):
        return pltpu.make_async_remote_copy(
            src_ref=src, dst_ref=dst, send_sem=send, recv_sem=recv,
            device_id=stream_device(k), device_id_type=MESH,
        )

    def blank(x, inside, ranges):
        for lo, hi in ranges:
            def plane(n, carry):
                x[n] = jnp.where(inside(n), x[n], 0.0)
                return carry

            lax.fori_loop(lo, hi, plane, 0)

    copies = [
        exchange(-1, x1.at[pl.ds(H1, H1)], x1.at[pl.ds(H1 + N1, H1)], send_1.at[0], recv_1.at[0]),
        exchange(1, x1.at[pl.ds(N1, H1)], x1.at[pl.ds(0, H1)], send_1.at[1], recv_1.at[1]),
    ]
    for copy in copies:
        copy.start()
    for copy in copies:
        copy.wait()
    blank(x1, in1, [(0, H1), (H1 + N1, N1 + 2 * H1)])
    lev1, lev2, lev3 = Level(8, SIDE, 1), Level(8, SIDE, 2), Level(8, SIDE, 4)
    weights(
        lev1, DIFFUSION_NUMBER / 4, 1, N1 + 2 * H1 - 1, lambda n: x1[n, 3], lambda c, n: x1[n, c],
        in1, g1, iw1, s1,
    )
    sweep(lev1, 2, N1 + 2 * H1 - 2, g1, s1, s1, a1)

    def down_1(m, carry):
        n = H1 + 2 * m
        first = residual(lev1, n, g1, iw1, s1, a1)
        second = residual(lev1, n + 1, g1, iw1, s1, a1)
        for c in range(3):
            x2[H2 + m, c] = 0.125 * pair_sum(first[c] + second[c], 1)
        x2[H2 + m, 3] = 0.125 * pair_sum(x1[n, 3] + x1[n + 1, 3], 1)
        return carry

    lax.fori_loop(0, N2, down_1, 0)

    row8 = lax.broadcasted_iota(jnp.int32, (8, LANES), 0)
    lane8 = lax.broadcasted_iota(jnp.int32, (8, LANES), 1)
    place2 = lax.rem(row8, 2) * 2 + lax.rem(lane8, 2)
    place3 = lax.rem(row8, 4) * 4 + lax.rem(lane8, 4)

    def pack_2(m, carry):
        made = x2[H2 + m, 0]
        for f in range(1, 4):
            made = jnp.where(place2 == f, x2[H2 + m, f], made)
        pk2[H2 + m] = made
        return carry

    lax.fori_loop(0, N2, pack_2, 0)
    copies = [
        exchange(-1, pk2.at[pl.ds(H2, H2)], pk2.at[pl.ds(H2 + N2, H2)], send_2.at[0], recv_2.at[0]),
        exchange(1, pk2.at[pl.ds(N2, H2)], pk2.at[pl.ds(0, H2)], send_2.at[1], recv_2.at[1]),
    ]
    for copy in copies:
        copy.start()
    for copy in copies:
        copy.wait()

    def unpack_2(n, carry):
        packed = jnp.where(in2(n), pk2[n], 0.0)
        for f in range(4):
            x2[n, f] = pair_sum(jnp.where(place2 == f, packed, 0.0), 1)
        return carry

    lax.fori_loop(0, H2, unpack_2, 0)
    lax.fori_loop(H2 + N2, N2 + 2 * H2, unpack_2, 0)
    weights(
        lev2, DIFFUSION_NUMBER / 16, 1, N2 + 2 * H2 - 1, lambda n: x2[n, 3], lambda c, n: x2[n, c],
        in2, g2, iw2, s2,
    )
    sweep(lev2, 2, N2 + 2 * H2 - 2, g2, s2, s2, a2)

    def down_2(m, carry):
        n = H2 + 2 * m
        first = residual(lev2, n, g2, iw2, s2, a2)
        second = residual(lev2, n + 1, g2, iw2, s2, a2)
        for c in range(3):
            x3[H3 + m, c] = 0.125 * pair_sum(first[c] + second[c], 2)
        x3[H3 + m, 3] = 0.125 * pair_sum(x2[n, 3] + x2[n + 1, 3], 2)
        return carry

    lax.fori_loop(0, N3, down_2, 0)

    made = x3[H3, 0]
    for m in range(N3):
        for f in range(4):
            if m or f:
                made = jnp.where(place3 == 4 * m + f, x3[H3 + m, f], made)
    pk3[REACH] = made
    copies = [
        exchange(k, pk3.at[REACH], pk3.at[REACH - k], send_3.at[i], recv_3.at[i])
        for i, k in enumerate(hops)
    ]
    for copy in copies:
        copy.start()
    for copy in copies:
        copy.wait()

    def unpack_3(b, carry):
        packed = pk3[b]
        for m in range(N3):
            n = N3 * b + m
            for f in range(4):
                one = jnp.where((place3 == 4 * m + f) & in3(n), packed, 0.0)
                x3[n, f] = pair_sum(pair_sum(one, 1), 2)
        return carry

    lax.fori_loop(0, REACH, unpack_3, 0)
    lax.fori_loop(REACH + 1, 2 * REACH + 1, unpack_3, 0)
    planes3 = N3 + 2 * H3
    lo = H3 - 2 - (BOTTOM - 1)
    weights(
        lev3, DIFFUSION_NUMBER / 64, lo, planes3 - lo, lambda n: x3[n, 3], lambda c, n: x3[n, c],
        in3, g3, iw3, s3,
    )
    b3 = [x3.at[:, c] for c in range(3)]
    src = s3
    for turn in range(1, BOTTOM):
        dst = a3 if turn % 2 else b3
        sweep(lev3, lo + turn, planes3 - lo - turn, g3, s3, src, dst)
        src = dst
    b2 = [x2.at[:, c] for c in range(3)]

    def add_3(n, carry):
        m = H3 - 2 + (n - (H2 - 4)) // 2
        for c in range(3):
            a2[c][n] = a2[c][n] + src[c][m]
        return carry

    lax.fori_loop(2, N2 + 2 * H2 - 2, add_3, 0)
    sweep(lev2, 3, N2 + 2 * H2 - 3, g2, s2, a2, b2)
    sweep(lev2, 4, N2 + 2 * H2 - 4, g2, s2, b2, a2)
    b1 = [x1.at[:, c] for c in range(3)]

    def add_2(n, carry):
        m = H2 - 2 + (n - (H1 - 4)) // 2
        for c in range(3):
            a1[c][n] = a1[c][n] + a2[c][m]
        return carry

    lax.fori_loop(2, N1 + 2 * H1 - 2, add_2, 0)
    sweep(lev1, 3, N1 + 2 * H1 - 3, g1, s1, a1, b1)
    sweep(lev1, 4, N1 + 2 * H1 - 4, g1, s1, b1, a1)
    wide = N1 + 2
    for c in range(3):
        coarse = a1[c][pl.ds(H1 - 1, wide)].reshape(wide * 8, LANES)
        for jh in (0, 1):
            half[c, jh] = jnp.dot(
                coarse, up_m[jh], precision=HIGHEST, preferred_element_type=F32
            ).reshape(wide, 8, LANES)

    def add_1(m, carry):
        for c in range(3):
            for jh in (0, 1):
                for twin in (0, 1):
                    tmp[c, pl.ds(16 * jh + twin, 8, stride=2), :] = half[c, jh, m]
            for twin in (0, 1):
                n = H0 - 2 + 2 * m + twin
                b0[c][n] = b0[c][n] + tmp[c]
        return carry

    lax.fori_loop(0, wide, add_1, 0)
    sweep(fine, 3, N0 + 2 * H0 - 3, g0, s0, b0, a0)
    sweep(fine, 4, N0 + 2 * H0 - 4, g0, s0, a0, (o_0, o_1, o_2), shift=H0)


def vcycle(fields):
    vmem = pl.BlockSpec(memory_space=pltpu.VMEM)

    def level_scratch(planes, rows, copies):
        one = pltpu.VMEM((planes, rows, LANES), F32)
        return [pltpu.VMEM((6, planes, rows, LANES), F32), one] + [one] * (3 * copies)

    n0, n1, n2, n3 = N0 + 2 * H0, N1 + 2 * H1, N2 + 2 * H2, N3 + 2 * H3
    return pl.pallas_call(
        vcycle_kernel,
        out_shape=[jax.ShapeDtypeStruct((N0, SIDE, LANES), F32)] * 3,
        in_specs=[vmem] * 4,
        out_specs=[vmem] * 3,
        scratch_shapes=level_scratch(n0, SIDE, 3)
        + [pltpu.VMEM((4, SIDE, LANES), F32), pltpu.VMEM((4, 2, N1 + 2, 8, LANES), F32)]
        + [pltpu.VMEM((n1, 4, 8, LANES), F32)] + level_scratch(n1, 8, 2)
        + [pltpu.VMEM((n2, 4, 8, LANES), F32)] + level_scratch(n2, 8, 2)
        + [pltpu.VMEM((n3, 4, 8, LANES), F32)] + level_scratch(n3, 8, 2)
        + [pltpu.VMEM((n2, 8, LANES), F32), pltpu.VMEM((2 * REACH + 1, 8, LANES), F32)]
        + [pltpu.SemaphoreType.DMA((2,))] * 4
        + [pltpu.SemaphoreType.DMA((2 * REACH,))] * 2,
        compiler_params=pltpu.CompilerParams(
            collective_id=1, has_side_effects=True, vmem_limit_bytes=VMEM_LIMIT
        ),
        name="vcycle",
    )(*fields)


def blocks_kernel(e_0, e_1, e_2, out_ref):
    for c, e in enumerate((e_0, e_1, e_2)):
        def tile(t, carry):
            parts = [e[pl.ds(4 * t + jj, SIDE, stride=SIDE), :] for jj in range(4)]
            turned = jnp.concatenate(parts, axis=0).T
            lanes = pl.ds(multiple(t * LANES, LANES), LANES)
            for at, slot in enumerate(LANE_SLOTS):
                out_ref[slot, c, :, lanes] = turned[SIDE * at : SIDE * at + SIDE]
            return carry

        lax.fori_loop(0, 8, tile, 0)


def to_blocks(planes):
    vmem = pl.BlockSpec(memory_space=pltpu.VMEM)
    return pl.pallas_call(
        blocks_kernel,
        out_shape=jax.ShapeDtypeStruct((4, 3, SIDE, SIDE * SIDE), F32),
        in_specs=[vmem] * 3,
        out_specs=vmem,
        compiler_params=pltpu.CompilerParams(vmem_limit_bytes=VMEM_LIMIT),
        name="to_blocks",
    )(*[p.reshape(SIDE * SIDE, LANES) for p in planes])


def solution(mesh):
    n_dev = mesh.shape["dev"]

    def local(velocity_old, viscosity_old, source):
        fields = regrid(n_dev, source, velocity_old, viscosity_old)
        return to_blocks(vcycle(fields))

    return jax.shard_map(
        local,
        mesh=mesh,
        in_specs=(P(("grp", "dev"), None, None, None), P(("grp", "dev"), None, None), P()),
        out_specs=P(("grp", "dev"), None, None, None),
        check_vma=False,
    )
```

```python
import functools

import jax
import jax.numpy as jnp
from jax import lax
from jax.experimental import pallas as pl
from jax.experimental.pallas import tpu as pltpu
from jax.sharding import PartitionSpec as P

F32 = jnp.float32
SIDE = 32
LANES = 128
DIFFUSION_NUMBER = 1000.0
RELAX = 0.8
BOTTOM = 8
LANE_SLOTS = (0, 2, 1, 3)
H0, H1, H2 = 4, 5, 6
N0, N1, N2, N3 = 32, 16, 8, 4
REACH = 3
H3 = REACH * N3
VMEM_LIMIT = 48 * 1024 * 1024
MESH = pl.DeviceIdType.MESH
HIGHEST = lax.Precision.HIGHEST


def positions():
    grp, dev = lax.axis_index("grp"), lax.axis_index("dev")
    n_grp, n_dev = lax.axis_size("grp"), lax.axis_size("dev")
    return grp, dev, n_grp, n_dev


def stream_device(offset):
    grp, dev, n_grp, n_dev = positions()
    at = lax.rem(grp * n_dev + dev + offset + n_grp * n_dev, n_grp * n_dev)
    return (at // n_dev, lax.rem(at, n_dev))


TOP = 8
TALL = SIDE + 2 * TOP
BODY = slice(TOP, TOP + SIDE)


def multiple(value, of):
    return pl.multiple_of(value, of)


def put(ref, n, v):
    ref[n, BODY] = v
    ref[n, :TOP] = pltpu.roll(v[SIDE - TOP :], LANES // 2, 1)
    ref[n, TOP + SIDE :] = pltpu.roll(v[:TOP], LANES // 2, 1)


def fine_beside(ref, n, v):
    return (
        pltpu.roll(v, 1, 1),
        pltpu.roll(v, LANES - 1, 1),
        ref[n, TOP - 1 : TOP + SIDE - 1],
        ref[n, TOP + 1 : TOP + SIDE + 1],
    )


def steps(lo, hi, most, body):
    size = max(t for t in range(1, most + 1) if (hi - lo) % t == 0)

    def step(i, carry):
        body([lo + size * i + t for t in range(size)])
        return carry

    if size == hi - lo:
        step(0, 0)
    else:
        lax.fori_loop(0, (hi - lo) // size, step, 0)


class Level:
    def __init__(self, rows, wide, high, d):
        self.wide, self.d = wide, d
        row = lax.broadcasted_iota(jnp.int32, (rows, LANES), 0)
        lane = lax.broadcasted_iota(jnp.int32, (rows, LANES), 1)
        deep = lax.rem(lane, high)
        self.ok_zm = deep >= d
        self.ok_zp = deep < high - d
        self.ok_ym = (row >= d) | (lane >= wide)
        self.ok_yp = (row < rows - d) | (lane < LANES - wide)
        self.wrap_m = row < d
        self.wrap_p = row >= rows - d

    def beside(self, ref, n, a):
        wide, d = self.wide, self.d
        zm = pltpu.roll(a, d, 1)
        zp = pltpu.roll(a, LANES - d, 1)
        ym = pltpu.roll(a, d, 0)
        ym = jnp.where(self.wrap_m, pltpu.roll(ym, wide, 1), ym)
        yp = pltpu.roll(a, 8 - d, 0)
        yp = jnp.where(self.wrap_p, pltpu.roll(yp, LANES - wide, 1), yp)
        return zm, zp, ym, yp


class Fine(Level):
    def beside(self, ref, n, a):
        return fine_beside(ref, n, a)


def spread_rows(a, d):
    row = lax.broadcasted_iota(jnp.int32, a.shape, 0)
    first = lax.rem(row // d, 2) == 0
    return a + jnp.where(first, pltpu.roll(a, a.shape[0] - d, 0), pltpu.roll(a, d, 0))


def spread_lanes(a, d):
    lane = lax.broadcasted_iota(jnp.int32, a.shape, 1)
    first = lax.rem(lane // d, 2) == 0
    return a + jnp.where(first, pltpu.roll(a, LANES - d, 1), pltpu.roll(a, d, 1))


def pair_sum(a, d):
    return spread_lanes(spread_rows(a, d), d)


def weights(level, coef, lo, hi, most, nu_ref, at, inside, g_ref, w_ref, iw_ref):
    def planes(ns):
        made = []
        for n in ns:
            nu = nu_ref[n, at]
            xm, xp = nu_ref[n - 1, at], nu_ref[n + 1, at]
            zm, zp, ym, yp = level.beside(nu_ref, n, nu)
            zm = jnp.where(level.ok_zm, zm, 0.0)
            zp = jnp.where(level.ok_zp, zp, 0.0)
            ym = jnp.where(level.ok_ym, ym, 0.0)
            yp = jnp.where(level.ok_yp, yp, 0.0)
            total = 6.0 * nu + ((xm + xp) + (zm + zp) + (ym + yp))
            diag = 1.0 + (0.5 * coef) * total
            w = RELAX / diag
            k = w * jnp.where(inside(n), 0.5 * coef, 0.0)
            made.append(
                (
                    n, w, diag * (1.0 / RELAX), k * (nu + xm), k * (nu + xp),
                    jnp.where(level.ok_zm, k * (nu + zm), 0.0),
                    jnp.where(level.ok_zp, k * (nu + zp), 0.0),
                    jnp.where(level.ok_ym, k * (nu + ym), 0.0),
                    jnp.where(level.ok_yp, k * (nu + yp), 0.0),
                )
            )
        for n, w, iw, *g in made:
            w_ref[n] = w
            iw_ref[n] = iw
            for i in range(6):
                g_ref[i, n] = g[i]

    steps(lo, hi, most, planes)


def gathered(level, g, src, at, n, v):
    zm, zp, ym, yp = level.beside(src, n, v)
    return (
        (g[0] * src[n - 1, at] + g[1] * src[n + 1, at])
        + (g[2] * zm + g[3] * zp)
        + (g[4] * ym + g[5] * yp)
    )


ALL = slice(None)


def sweep(level, lo, hi, most, g_ref, s_refs, srcs, store, at=ALL):
    def planes(ns):
        made = []
        for n in ns:
            g = [g_ref[i, n] for i in range(6)]
            for c, (s, src) in enumerate(zip(s_refs, srcs)):
                v = src[n, at]
                made.append(
                    (c, n, (1.0 - RELAX) * v + (s[n] + gathered(level, g, src, at, n, v)))
                )
        for c, n, v in made:
            store(c, n, v)

    steps(lo, hi, most, planes)


def storing(refs):
    def store(c, n, v):
        refs[c][n] = v

    return store


def residual(level, n, g_ref, iw_ref, s_refs, srcs, at=ALL):
    g = [g_ref[i, n] for i in range(6)]
    made = []
    for s, src in zip(s_refs, srcs):
        v = src[n, at]
        made.append(iw_ref[n] * ((s[n] + gathered(level, g, src, at, n, v)) - RELAX * v))
    return made


def names_of_scratch(n_dev):
    each = SIDE // n_dev
    n0, n1, n2, n3 = N0 + 2 * H0, N1 + 2 * H1, N2 + 2 * H2, N3 + 2 * H3

    def vmem(*shape):
        return pltpu.VMEM((*shape, LANES), F32)

    def dma(*shape):
        return pltpu.SemaphoreType.DMA(shape)

    named = {"vis": pltpu.VMEM((4, SIDE, SIDE * SIDE), F32)}
    for c in range(3):
        named[f"vel{c}"] = pltpu.VMEM((4, SIDE, SIDE * SIDE), F32)
    for f in range(4):
        named[f"stage{f}"] = vmem(SIDE * SIDE)
        named[f"mid{f}"] = vmem(n_dev, each * SIDE)
        named[f"asm{f}"] = vmem(n_dev, each, SIDE)
        named[f"grid{f}"] = vmem(n0, TALL)
    named |= {"g0": vmem(6, n0, SIDE), "w0": vmem(n0, SIDE), "iw0": vmem(n0, SIDE)}
    for c in range(3):
        named[f"s0{c}"] = vmem(n0, SIDE)
        named[f"a0{c}"] = vmem(n0, TALL)
        named[f"b0{c}"] = vmem(n0, TALL)
    named |= {"tmp": vmem(3 * 3, SIDE), "half": vmem(4, 2, N1 + 2, 8)}
    for level, n in ((1, n1), (2, n2), (3, n3)):
        named |= {
            f"nu{level}": vmem(n, 8), f"x{level}": vmem(n, 3, 8), f"g{level}": vmem(6, n, 8),
            f"w{level}": vmem(n, 8), f"iw{level}": vmem(n, 8),
        }
        for c in range(3):
            for kind in "sab":
                named[f"{kind}{level}{c}"] = vmem(n, 8)
    named |= {
        "pk2": vmem(n2, 8), "pk3": vmem(2 * REACH + 1, 8), "in_sem": dma(4),
        "send_1": dma(4), "recv_1": dma(4), "send_2": dma(4), "recv_2": dma(4),
        "send_h": dma(4, 2), "recv_h": dma(4, 2), "send_e": dma(5, 2), "recv_e": dma(5, 2),
        "send_n3": dma(2 * REACH), "recv_n3": dma(2 * REACH),
        "send_r3": dma(2 * REACH), "recv_r3": dma(2 * REACH),
    }
    return named


def whole_kernel(names, source_ref, vel_hbm, vis_hbm, o_0, o_1, o_2, *scratch):
    r = dict(zip(names, scratch))
    grp, dev, n_grp, n_dev = positions()
    at = grp * n_dev + dev
    count = n_grp * n_dev
    each = SIDE // n_dev
    rows = each * SIDE
    hops = [k for k in range(-REACH, REACH + 1) if k]
    stages, mids = [r[f"stage{f}"] for f in range(4)], [r[f"mid{f}"] for f in range(4)]
    asms, grids = [r[f"asm{f}"] for f in range(4)], [r[f"grid{f}"] for f in range(4)]
    inputs = [r["vis"]] + [r[f"vel{c}"] for c in range(3)]

    def three(kind, level):
        return [r[f"{kind}{level}{c}"] for c in range(3)]

    loads = [pltpu.make_async_copy(vis_hbm, inputs[0], r["in_sem"].at[0])]
    loads += [
        pltpu.make_async_copy(vel_hbm.at[:, c], inputs[1 + c], r["in_sem"].at[1 + c])
        for c in range(3)
    ]
    for load in loads:
        load.start()
    barrier = pltpu.get_barrier_semaphore()

    def greet(t, carry):
        pl.semaphore_signal(
            barrier, inc=1, device_id=(grp, lax.rem(dev + t, n_dev)), device_id_type=MESH
        )
        return carry

    lax.fori_loop(1, n_dev, greet, 0)
    for k in hops:
        pl.semaphore_signal(barrier, inc=1, device_id=stream_device(k), device_id_type=MESH)

    def transpose_field(f):
        def tile(t, carry):
            lanes = pl.ds(multiple(t * LANES, LANES), LANES)
            turned = jnp.concatenate([inputs[f][b, :, lanes] for b in LANE_SLOTS], axis=0).T
            for jj in range(4):
                stages[f][pl.ds(4 * t + jj, SIDE, stride=SIDE), :] = turned[
                    SIDE * jj : SIDE * jj + SIDE
                ]
            return carry

        lax.fori_loop(0, 8, tile, 0)

    def spread(f):
        def send(t, carry):
            to = lax.rem(dev + t, n_dev)
            pltpu.make_async_remote_copy(
                src_ref=stages[f].at[pl.ds(multiple(to * rows, rows), rows)],
                dst_ref=mids[f].at[dev],
                send_sem=r["send_1"].at[f],
                recv_sem=r["recv_1"].at[f],
                device_id=(grp, to),
                device_id_type=MESH,
            ).start()
            return carry

        pltpu.make_async_copy(
            stages[f].at[pl.ds(multiple(dev * rows, rows), rows)], mids[f].at[dev],
            r["recv_1"].at[f],
        ).start()
        lax.fori_loop(1, n_dev, send, 0)

    group_of_lane = lax.broadcasted_iota(jnp.int32, (rows, LANES), 1) // SIDE

    def collect(f):
        pltpu.make_async_copy(mids[f], mids[f], r["recv_1"].at[f]).wait()
        mine = grids[f].at[pl.ds(H0 + dev * each, each), pl.ds(TOP, SIDE)]

        def assemble(to):
            base = (grp * n_dev + to) * 4
            made = None
            for place, slot in enumerate(LANE_SLOTS):
                old = lax.rem(source_ref[base + slot] // 4, n_dev)
                piece = mids[f][old]
                made = piece if made is None else jnp.where(group_of_lane == place, piece, made)
            asms[f][to] = made.reshape(each, SIDE, LANES)

        def send(t, carry):
            to = lax.rem(dev + t, n_dev)
            assemble(to)
            pltpu.make_async_remote_copy(
                src_ref=asms[f].at[to],
                dst_ref=mine,
                send_sem=r["send_2"].at[f],
                recv_sem=r["recv_2"].at[f],
                device_id=(grp, to),
                device_id_type=MESH,
            ).start()
            return carry

        lax.fori_loop(1, n_dev, send, 0)
        assemble(dev)
        pltpu.make_async_copy(asms[f].at[dev], mine, r["recv_2"].at[f]).start()

    def exchange(k, src, dst, send, recv):
        return pltpu.make_async_remote_copy(
            src_ref=src, dst_ref=dst, send_sem=send, recv_sem=recv,
            device_id=stream_device(k), device_id_type=MESH,
        )

    def start(copies):
        for copy in copies:
            copy.start()
        return copies

    def wait(copies):
        for copy in copies:
            copy.wait()

    def halos(x, own, halo, send, recv, *more):
        def part(lo):
            return x.at[(pl.ds(lo, halo), *more)]

        return [
            exchange(-1, part(halo), part(halo + own), send.at[0], recv.at[0]),
            exchange(1, part(own), part(0), send.at[1], recv.at[1]),
        ]

    def grid_halos(f):
        own = grids[f].at[pl.ds(H0, N0), pl.ds(TOP, SIDE)]
        pltpu.make_async_copy(own, own, r["recv_2"].at[f]).wait()
        body = pl.ds(TOP, SIDE)
        return start(halos(grids[f], N0, H0, r["send_h"].at[f], r["recv_h"].at[f], body))

    def grid_ready(f, copies):
        wait(copies)
        for edge, lo in ((0, 0), (count - 1, H0 + N0)):
            @pl.when(at == edge)
            def _():
                grids[f][pl.ds(lo, H0)] = jnp.zeros((H0, TALL, LANES), F32)

        def ghosts(ns):
            made = [(n, grids[f][n, BODY]) for n in ns]
            for n, v in made:
                grids[f][n, :TOP] = pltpu.roll(v[SIDE - TOP :], LANES // 2, 1)
                grids[f][n, TOP + SIDE :] = pltpu.roll(v[:TOP], LANES // 2, 1)

        steps(0, N0 + 2 * H0, 8, ghosts)

    def inside_of(own, halo):
        def inside(n):
            cell = at * own + n - halo
            return (cell >= 0) & (cell < count * own)

        return inside

    in0, in1 = inside_of(N0, H0), inside_of(N1, H1)
    in2, in3 = inside_of(N2, H2), inside_of(N3, H3)
    fine = Fine(SIDE, 2 * SIDE, 2 * SIDE, 1)
    lev1, lev2, lev3 = (Level(8, SIDE, SIDE, d) for d in (1, 2, 4))
    lane_f = lax.broadcasted_iota(jnp.int32, (LANES, LANES), 0)
    lane_c = lax.broadcasted_iota(jnp.int32, (LANES, LANES), 1)
    target = (lane_f // 64) * 64 + lax.rem(lane_f, 64) // 2
    down_m = [jnp.where(lane_c == target + 32 * jh, 0.5, 0.0).astype(F32) for jh in (0, 1)]
    target_t = (lane_c // 64) * 64 + lax.rem(lane_c, 64) // 2
    up_m = [jnp.where(lane_f == target_t + 32 * jh, 1.0, 0.0).astype(F32) for jh in (0, 1)]
    row8 = lax.broadcasted_iota(jnp.int32, (8, LANES), 0)
    lane8 = lax.broadcasted_iota(jnp.int32, (8, LANES), 1)
    tmp, half = r["tmp"], r["half"]

    def rows_halved(f, ms, totals):
        for i, total in enumerate(totals):
            tmp[i] = total
        made = [
            0.25 * (tmp[i, pl.ds(0, 16, stride=2), :] + tmp[i, pl.ds(1, 16, stride=2), :])
            for i in range(len(totals))
        ]
        for m, pairs in zip(ms, made):
            half[f, 0, m] = pairs[:8]
            half[f, 1, m] = pairs[8:]

    def lanes_halved(f):
        made = None
        for jh in (0, 1):
            part = jnp.dot(
                half[f, jh, :N1].reshape(N1 * 8, LANES), down_m[jh],
                precision=HIGHEST, preferred_element_type=F32,
            )
            made = part if made is None else made + part
        return made.reshape(N1, 8, LANES)

    def nu_pairs(ms):
        rows_halved(
            3, ms, [grids[0][H0 + 2 * m, BODY] + grids[0][H0 + 2 * m + 1, BODY] for m in ms]
        )

    def down_0(c):
        grid, s, a, b = grids[1 + c], r[f"s0{c}"], r[f"a0{c}"], r[f"b0{c}"]

        def first(ns):
            made = []
            for n in ns:
                g = [r["g0"][i, n] for i in range(6)]
                v = grid[n, BODY]
                scaled = r["w0"][n] * v
                made.append(
                    (n, scaled,
                     (1.0 - RELAX) * v + (scaled + gathered(fine, g, grid, BODY, n, v)))
                )
            for n, scaled, v in made:
                s[n] = scaled
                put(a, n, v)

        steps(1, N0 + 2 * H0 - 1, 2, first)
        sweep(
            fine, 2, N0 + 2 * H0 - 2, 2, r["g0"], [s], [a], lambda _, n, v: put(b, n, v), BODY
        )

        def pairs(ms):
            totals = []
            for m in ms:
                n = H0 + 2 * m
                [one] = residual(fine, n, r["g0"], r["iw0"], [s], [b], BODY)
                [two] = residual(fine, n + 1, r["g0"], r["iw0"], [s], [b], BODY)
                totals.append(one + two)
            rows_halved(c, ms, totals)

        steps(0, N1, 2, pairs)
        r["x1"][pl.ds(H1, N1), c] = lanes_halved(c)

    def blank(x, inside, ranges):
        for lo, hi in ranges:
            def planes(ns):
                made = [(n, jnp.where(inside(n), x[n], 0.0)) for n in ns]
                for n, v in made:
                    x[n] = v

            steps(lo, hi, 12, planes)

    def scaled(x, w, outs, lo, hi):
        def planes(ns):
            made = [(n, c, w[n] * x[n, c]) for n in ns for c in range(3)]
            for n, c, v in made:
                outs[c][n] = v

        steps(lo, hi, 8, planes)

    loads[0].wait()
    transpose_field(0)
    pl.semaphore_wait(barrier, n_dev - 1 + len(hops))
    spread(0)
    for f in range(1, 4):
        loads[f].wait()
        transpose_field(f)
        spread(f)
    for f in range(4):
        collect(f)

    grid_ready(0, grid_halos(0))
    weights(
        fine, DIFFUSION_NUMBER, 1, N0 + 2 * H0 - 1, 2, grids[0], BODY, in0, r["g0"], r["w0"],
        r["iw0"],
    )
    steps(0, N1, 4, nu_pairs)
    nu1, nu2, nu3 = r["nu1"], r["nu2"], r["nu3"]
    nu1[pl.ds(H1, N1)] = lanes_halved(3)
    moving = start(halos(nu1, N1, H1, r["send_e"].at[0], r["recv_e"].at[0]))
    waiting = grid_halos(1)

    wait(moving)
    blank(nu1, in1, [(0, H1), (H1 + N1, N1 + 2 * H1)])

    def nu_down(fine_nu, coarse_nu, halo_f, halo_c, d):
        def planes(ms):
            made = [
                (m, 0.125 * pair_sum(fine_nu[halo_f + 2 * m] + fine_nu[halo_f + 2 * m + 1], d))
                for m in ms
            ]
            for m, v in made:
                coarse_nu[halo_c + m] = v

        return planes

    steps(0, N2, 8, nu_down(nu1, nu2, H1, H2, 1))
    moving = start(halos(nu2, N2, H2, r["send_e"].at[1], r["recv_e"].at[1]))
    weights(
        lev1, DIFFUSION_NUMBER / 4, 1, N1 + 2 * H1 - 1, 6, nu1, ALL, in1, r["g1"], r["w1"], r["iw1"]
    )
    grid_ready(1, waiting)
    down_0(0)
    waiting = grid_halos(2)

    wait(moving)
    blank(nu2, in2, [(0, H2), (H2 + N2, N2 + 2 * H2)])
    steps(0, N3, 8, nu_down(nu2, nu3, H2, H3, 2))
    moving = start(
        [
            exchange(
                k, nu3.at[pl.ds(H3, N3)], nu3.at[pl.ds(H3 - k * N3, N3)],
                r["send_n3"].at[i], r["recv_n3"].at[i],
            )
            for i, k in enumerate(hops)
        ]
    )
    weights(
        lev2, DIFFUSION_NUMBER / 16, 1, N2 + 2 * H2 - 1, 6, nu2, ALL, in2, r["g2"], r["w2"],
        r["iw2"],
    )
    grid_ready(2, waiting)
    down_0(1)
    waiting = grid_halos(3)

    wait(moving)
    blank(nu3, in3, [(0, H3), (H3 + N3, N3 + 2 * H3)])
    planes3 = N3 + 2 * H3
    lo = H3 - 2 - (BOTTOM - 1)
    weights(
        lev3, DIFFUSION_NUMBER / 64, lo, planes3 - lo, 6, nu3, ALL, in3, r["g3"], r["w3"], r["iw3"]
    )
    grid_ready(3, waiting)
    down_0(2)

    x1, x2, x3 = r["x1"], r["x2"], r["x3"]
    s1, a1, b1 = three("s", 1), three("a", 1), three("b", 1)
    s2, a2, b2 = three("s", 2), three("a", 2), three("b", 2)
    s3, a3, b3 = three("s", 3), three("a", 3), three("b", 3)
    wait(start(halos(x1, N1, H1, r["send_e"].at[2], r["recv_e"].at[2])))
    blank(x1, in1, [(0, H1), (H1 + N1, N1 + 2 * H1)])
    scaled(x1, r["w1"], s1, 1, N1 + 2 * H1 - 1)
    sweep(lev1, 2, N1 + 2 * H1 - 2, 11, r["g1"], s1, s1, storing(a1))

    def down(level, ms, halo_f, halo_c, g, iw, s, a, x, d):
        made = []
        for m in ms:
            n = halo_f + 2 * m
            one = residual(level, n, g, iw, s, a)
            two = residual(level, n + 1, g, iw, s, a)
            for c in range(3):
                made.append((m, c, 0.125 * pair_sum(one[c] + two[c], d)))
        for m, c, v in made:
            x[halo_c + m, c] = v

    steps(0, N2, 4, lambda ms: down(lev1, ms, H1, H2, r["g1"], r["iw1"], s1, a1, x2, 1))

    place2 = lax.rem(row8, 2) * 2 + lax.rem(lane8, 2)
    pk2, pk3 = r["pk2"], r["pk3"]

    def pack_2(ms):
        made = []
        for m in ms:
            one = x2[H2 + m, 0]
            for c in (1, 2):
                one = jnp.where(place2 == c, x2[H2 + m, c], one)
            made.append((m, one))
        for m, one in made:
            pk2[H2 + m] = one

    steps(0, N2, 8, pack_2)
    wait(start(halos(pk2, N2, H2, r["send_e"].at[3], r["recv_e"].at[3])))

    def unpack_2(ns):
        made = []
        for n in ns:
            packed = jnp.where(in2(n), pk2[n], 0.0)
            for c in range(3):
                made.append((n, c, pair_sum(jnp.where(place2 == c, packed, 0.0), 1)))
        for n, c, v in made:
            x2[n, c] = v

    steps(0, H2, 6, unpack_2)
    steps(H2 + N2, N2 + 2 * H2, 6, unpack_2)
    scaled(x2, r["w2"], s2, 1, N2 + 2 * H2 - 1)
    sweep(lev2, 2, N2 + 2 * H2 - 2, 8, r["g2"], s2, s2, storing(a2))
    steps(0, N3, 4, lambda ms: down(lev2, ms, H2, H3, r["g2"], r["iw2"], s2, a2, x3, 2))

    row_of, lane_of = lax.rem(row8, 4), lax.rem(lane8, 4)
    made = None
    for m in range(N3):
        line = x3[H3 + m, 0]
        for c in (1, 2):
            line = jnp.where(lane_of == c, x3[H3 + m, c], line)
        made = line if made is None else jnp.where(row_of == m, line, made)
    pk3[REACH] = made
    wait(
        start(
            [
                exchange(k, pk3.at[REACH], pk3.at[REACH - k], r["send_r3"].at[i], r["recv_r3"].at[i])
                for i, k in enumerate(hops)
            ]
        )
    )

    def unpack_3(bs):
        made = []
        for b in bs:
            packed = pk3[b]
            for m in range(N3):
                n = N3 * b + m
                line = jnp.where((row_of == m) & in3(n), packed, 0.0)
                line = spread_rows(spread_rows(line, 1), 2)
                for c in range(3):
                    one = jnp.where(lane_of == c, line, 0.0)
                    made.append((n, c, spread_lanes(spread_lanes(one, 1), 2)))
        for n, c, v in made:
            x3[n, c] = v

    steps(0, REACH, 1, unpack_3)
    steps(REACH + 1, 2 * REACH + 1, 1, unpack_3)
    scaled(x3, r["w3"], s3, lo, planes3 - lo)
    src = s3
    for turn in range(1, BOTTOM):
        dst = a3 if turn % 2 else b3
        sweep(
            lev3, lo + turn, planes3 - lo - turn, 10, r["g3"], s3, src, storing(dst)
        )
        src = dst

    def add(bs, coarse, start_f, start_c):
        def pairs(ms):
            made = []
            for m in ms:
                for c in range(3):
                    more = coarse[c][start_c + m]
                    for twin in (0, 1):
                        n = start_f + 2 * m + twin
                        made.append((c, n, bs[c][n] + more))
            for c, n, v in made:
                bs[c][n] = v

        return pairs

    steps(0, (N2 + 8) // 2, 4, add(a2, src, H2 - 4, H3 - 2))
    sweep(lev2, 3, N2 + 2 * H2 - 3, 7, r["g2"], s2, a2, storing(b2))
    sweep(lev2, 4, N2 + 2 * H2 - 4, 6, r["g2"], s2, b2, storing(a2))
    steps(0, (N1 + 8) // 2, 4, add(a1, a2, H1 - 4, H2 - 2))
    sweep(lev1, 3, N1 + 2 * H1 - 3, 10, r["g1"], s1, a1, storing(b1))
    sweep(lev1, 4, N1 + 2 * H1 - 4, 9, r["g1"], s1, b1, storing(a1))

    wide = N1 + 2
    outs = (o_0, o_1, o_2)
    for c in range(3):
        coarse = a1[c][pl.ds(H1 - 1, wide)].reshape(wide * 8, LANES)
        for jh in (0, 1):
            half[c, jh] = jnp.dot(
                coarse, up_m[jh], precision=HIGHEST, preferred_element_type=F32
            ).reshape(wide, 8, LANES)

    for c in range(3):
        s, a, b = r[f"s0{c}"], r[f"a0{c}"], r[f"b0{c}"]

        def refined(ms, c=c, b=b):
            for i, m in enumerate(ms):
                for jh in (0, 1):
                    for twin in (0, 1):
                        tmp[3 * c + i, pl.ds(16 * jh + twin, 8, stride=2), :] = half[c, jh, m]
            made = []
            for i, m in enumerate(ms):
                for twin in (0, 1):
                    n = H0 - 2 + 2 * m + twin
                    made.append((n, b[n, BODY] + tmp[3 * c + i]))
            for n, v in made:
                put(b, n, v)

        steps(0, wide, 3, refined)
    s0, a0, b0 = three("s", 0), three("a", 0), three("b", 0)

    def to_a0(c, n, v):
        put(a0[c], n, v)

    def to_out(c, n, v):
        outs[c][n - H0] = v

    sweep(fine, 3, N0 + 2 * H0 - 3, 2, r["g0"], s0, b0, to_a0, BODY)
    sweep(fine, 4, N0 + 2 * H0 - 4, 2, r["g0"], s0, a0, to_out, BODY)

    for f in range(4):
        most = stages[f].at[pl.ds(0, (n_dev - 1) * rows)]
        pltpu.make_async_copy(most, most, r["send_1"].at[f]).wait()
        most = asms[f].at[pl.ds(0, n_dev - 1)]
        pltpu.make_async_copy(most, most, r["send_2"].at[f]).wait()


def whole(n_dev, source, velocity_old, viscosity_old):
    vmem = pl.BlockSpec(memory_space=pltpu.VMEM)
    anywhere = pl.BlockSpec(memory_space=pl.ANY)
    named = names_of_scratch(n_dev)
    return pl.pallas_call(
        functools.partial(whole_kernel, tuple(named)),
        out_shape=[jax.ShapeDtypeStruct((N0, SIDE, LANES), F32)] * 3,
        in_specs=[pl.BlockSpec(memory_space=pltpu.SMEM), anywhere, anywhere],
        out_specs=[vmem] * 3,
        scratch_shapes=list(named.values()),
        compiler_params=pltpu.CompilerParams(
            collective_id=0, has_side_effects=True, vmem_limit_bytes=VMEM_LIMIT
        ),
        name="whole",
    )(source, velocity_old, viscosity_old)


def blocks_kernel(e_0, e_1, e_2, out_ref):
    for c, e in enumerate((e_0, e_1, e_2)):
        def tile(t, carry):
            parts = [e[pl.ds(4 * t + jj, SIDE, stride=SIDE), :] for jj in range(4)]
            turned = jnp.concatenate(parts, axis=0).T
            lanes = pl.ds(multiple(t * LANES, LANES), LANES)
            for at, slot in enumerate(LANE_SLOTS):
                out_ref[slot, c, :, lanes] = turned[SIDE * at : SIDE * at + SIDE]
            return carry

        lax.fori_loop(0, 8, tile, 0)


def to_blocks(planes):
    vmem = pl.BlockSpec(memory_space=pltpu.VMEM)
    return pl.pallas_call(
        blocks_kernel,
        out_shape=jax.ShapeDtypeStruct((4, 3, SIDE, SIDE * SIDE), F32),
        in_specs=[vmem] * 3,
        out_specs=vmem,
        compiler_params=pltpu.CompilerParams(vmem_limit_bytes=VMEM_LIMIT),
        name="to_blocks",
    )(*[p.reshape(SIDE * SIDE, LANES) for p in planes])


def solution(mesh):
    n_dev = mesh.shape["dev"]

    def local(velocity_old, viscosity_old, source):
        return to_blocks(whole(n_dev, source, velocity_old, viscosity_old))

    return jax.shard_map(
        local,
        mesh=mesh,
        in_specs=(P(("grp", "dev"), None, None, None), P(("grp", "dev"), None, None), P()),
        out_specs=P(("grp", "dev"), None, None, None),
        check_vma=False,
    )
```

```python
import functools

import jax
import jax.numpy as jnp
from jax import lax
from jax.experimental import pallas as pl
from jax.experimental.pallas import tpu as pltpu
from jax.sharding import PartitionSpec as P

F32 = jnp.float32
SIDE = 32
LANES = 128
DIFFUSION_NUMBER = 1000.0
RELAX = 0.8
BOTTOM = 8
LANE_SLOTS = (0, 2, 1, 3)
ANY = 64
H0, H1, H2 = 4, 5, 6
N0, N1, N2, N3 = 32, 16, 8, 4
REACH = 3
H3 = REACH * N3
VMEM_LIMIT = 48 * 1024 * 1024
MESH = pl.DeviceIdType.MESH
HIGHEST = lax.Precision.HIGHEST


def positions():
    grp, dev = lax.axis_index("grp"), lax.axis_index("dev")
    n_grp, n_dev = lax.axis_size("grp"), lax.axis_size("dev")
    return grp, dev, n_grp, n_dev


def stream_device(offset):
    grp, dev, n_grp, n_dev = positions()
    at = lax.rem(grp * n_dev + dev + offset + n_grp * n_dev, n_grp * n_dev)
    return (at // n_dev, lax.rem(at, n_dev))


TOP = 8
TALL = SIDE + 2 * TOP
BODY = slice(TOP, TOP + SIDE)


def multiple(value, of):
    return pl.multiple_of(value, of)


def put(ref, n, v):
    ref[n, BODY] = v
    ref[n, :TOP] = pltpu.roll(v[SIDE - TOP :], LANES // 2, 1)
    ref[n, TOP + SIDE :] = pltpu.roll(v[:TOP], LANES // 2, 1)


def fine_beside(ref, n, v):
    return (
        pltpu.roll(v, 1, 1),
        pltpu.roll(v, LANES - 1, 1),
        ref[n, TOP - 1 : TOP + SIDE - 1],
        ref[n, TOP + 1 : TOP + SIDE + 1],
    )


def steps(lo, hi, most, body):
    count = hi - lo
    size = -(-count // -(-count // most))
    full, rest = divmod(count, size)

    def step(i, carry):
        body([lo + size * i + t for t in range(size)])
        return carry

    if full == 1:
        body(list(range(lo, lo + size)))
    else:
        lax.fori_loop(0, full, step, 0)
    if rest:
        body(list(range(hi - rest, hi)))


class Level:
    def __init__(self, rows, wide, high, d):
        self.wide, self.d = wide, d
        row = lax.broadcasted_iota(jnp.int32, (rows, LANES), 0)
        lane = lax.broadcasted_iota(jnp.int32, (rows, LANES), 1)
        deep = lax.rem(lane, high)
        self.ok_zm = deep >= d
        self.ok_zp = deep < high - d
        self.ok_ym = (row >= d) | (lane >= wide)
        self.ok_yp = (row < rows - d) | (lane < LANES - wide)
        self.wrap_m = row < d
        self.wrap_p = row >= rows - d

    def beside(self, ref, n, a):
        wide, d = self.wide, self.d
        zm = pltpu.roll(a, d, 1)
        zp = pltpu.roll(a, LANES - d, 1)
        ym = pltpu.roll(a, d, 0)
        ym = jnp.where(self.wrap_m, pltpu.roll(ym, wide, 1), ym)
        yp = pltpu.roll(a, 8 - d, 0)
        yp = jnp.where(self.wrap_p, pltpu.roll(yp, LANES - wide, 1), yp)
        return zm, zp, ym, yp


class Fine(Level):
    def beside(self, ref, n, a):
        return fine_beside(ref, n, a)


def spread_rows(a, d):
    row = lax.broadcasted_iota(jnp.int32, a.shape, 0)
    first = lax.rem(row // d, 2) == 0
    return a + jnp.where(first, pltpu.roll(a, a.shape[0] - d, 0), pltpu.roll(a, d, 0))


def spread_lanes(a, d):
    lane = lax.broadcasted_iota(jnp.int32, a.shape, 1)
    first = lax.rem(lane // d, 2) == 0
    return a + jnp.where(first, pltpu.roll(a, LANES - d, 1), pltpu.roll(a, d, 1))


def pair_sum(a, d):
    return spread_lanes(spread_rows(a, d), d)


def weights(level, coef, lo, hi, most, nu_ref, at, inside, g_ref, w_ref, iw_ref):
    def planes(ns):
        made = []
        for n in ns:
            nu = nu_ref[n, at]
            xm, xp = nu_ref[n - 1, at], nu_ref[n + 1, at]
            zm, zp, ym, yp = level.beside(nu_ref, n, nu)
            zm = jnp.where(level.ok_zm, zm, 0.0)
            zp = jnp.where(level.ok_zp, zp, 0.0)
            ym = jnp.where(level.ok_ym, ym, 0.0)
            yp = jnp.where(level.ok_yp, yp, 0.0)
            total = 6.0 * nu + ((xm + xp) + (zm + zp) + (ym + yp))
            diag = 1.0 + (0.5 * coef) * total
            w = RELAX / diag
            k = w * jnp.where(inside(n), 0.5 * coef, 0.0)
            made.append(
                (
                    n, w, diag * (1.0 / RELAX), k * (nu + xm), k * (nu + xp),
                    jnp.where(level.ok_zm, k * (nu + zm), 0.0),
                    jnp.where(level.ok_zp, k * (nu + zp), 0.0),
                    jnp.where(level.ok_ym, k * (nu + ym), 0.0),
                    jnp.where(level.ok_yp, k * (nu + yp), 0.0),
                )
            )
        for n, w, iw, *g in made:
            w_ref[n] = w
            iw_ref[n] = iw
            for i in range(6):
                g_ref[i, n] = g[i]

    steps(lo, hi, most, planes)


def gathered(level, g, src, at, n, v):
    zm, zp, ym, yp = level.beside(src, n, v)
    return (
        (g[0] * src[n - 1, at] + g[1] * src[n + 1, at])
        + (g[2] * zm + g[3] * zp)
        + (g[4] * ym + g[5] * yp)
    )


ALL = slice(None)


def sweep(level, lo, hi, most, g_ref, s_refs, srcs, store, at=ALL):
    def planes(ns):
        made = []
        for n in ns:
            g = [g_ref[i, n] for i in range(6)]
            for c, (s, src) in enumerate(zip(s_refs, srcs)):
                v = src[n, at]
                made.append(
                    (c, n, (1.0 - RELAX) * v + (s[n] + gathered(level, g, src, at, n, v)))
                )
        for c, n, v in made:
            store(c, n, v)

    steps(lo, hi, most, planes)


def storing(refs):
    def store(c, n, v):
        refs[c][n] = v

    return store


def residual(level, n, g_ref, iw_ref, s_refs, srcs, at=ALL):
    g = [g_ref[i, n] for i in range(6)]
    made = []
    for s, src in zip(s_refs, srcs):
        v = src[n, at]
        made.append(iw_ref[n] * ((s[n] + gathered(level, g, src, at, n, v)) - RELAX * v))
    return made


def names_of_scratch(n_dev):
    each = SIDE // n_dev
    n0, n1, n2, n3 = N0 + 2 * H0, N1 + 2 * H1, N2 + 2 * H2, N3 + 2 * H3

    def vmem(*shape):
        return pltpu.VMEM((*shape, LANES), F32)

    def dma(*shape):
        return pltpu.SemaphoreType.DMA(shape)

    named = {"vis": pltpu.VMEM((4, SIDE, SIDE * SIDE), F32)}
    for c in range(3):
        named[f"vel{c}"] = pltpu.VMEM((4, SIDE, SIDE * SIDE), F32)
    for f in range(4):
        named[f"stage{f}"] = vmem(SIDE * SIDE)
        named[f"mid{f}"] = vmem(n_dev, each * SIDE)
        named[f"asm{f}"] = vmem(n_dev, each, SIDE)
        named[f"grid{f}"] = vmem(n0, TALL)
    named |= {"g0": vmem(6, n0, SIDE), "w0": vmem(n0, SIDE), "iw0": vmem(n0, SIDE)}
    for c in range(3):
        named[f"s0{c}"] = vmem(n0, SIDE)
        named[f"a0{c}"] = vmem(n0, TALL)
        named[f"b0{c}"] = vmem(n0, TALL)
    named |= {"tmp": vmem(9, SIDE), "half": vmem(4, 2, N1 + 2, 8)}
    for level, n in ((1, n1), (2, n2), (3, n3)):
        named |= {
            f"nu{level}": vmem(n, 8), f"x{level}": vmem(n, 3, 8), f"g{level}": vmem(6, n, 8),
            f"w{level}": vmem(n, 8), f"iw{level}": vmem(n, 8),
        }
        for c in range(3):
            for kind in "sab":
                named[f"{kind}{level}{c}"] = vmem(n, 8)
    named |= {
        "pk2": vmem(n2, 8), "pk3": vmem(2 * REACH + 1, 8), "in_sem": dma(4),
        "send_1": dma(4), "recv_1": dma(4), "send_2": dma(4), "recv_2": dma(4),
        "send_h": dma(4, 2), "recv_h": dma(4, 2), "send_e": dma(5, 2), "recv_e": dma(5, 2),
        "send_n3": dma(2 * REACH), "recv_n3": dma(2 * REACH),
        "send_r3": dma(2 * REACH), "recv_r3": dma(2 * REACH),
    }
    return named


def whole_kernel(names, source_ref, vel_hbm, vis_hbm, o_0, o_1, o_2, *scratch):
    r = dict(zip(names, scratch))
    grp, dev, n_grp, n_dev = positions()
    at = grp * n_dev + dev
    count = n_grp * n_dev
    each = SIDE // n_dev
    rows = each * SIDE
    hops = [k for k in range(-REACH, REACH + 1) if k]
    stages, mids = [r[f"stage{f}"] for f in range(4)], [r[f"mid{f}"] for f in range(4)]
    asms, grids = [r[f"asm{f}"] for f in range(4)], [r[f"grid{f}"] for f in range(4)]
    inputs = [r["vis"]] + [r[f"vel{c}"] for c in range(3)]

    def three(kind, level):
        return [r[f"{kind}{level}{c}"] for c in range(3)]

    loads = [pltpu.make_async_copy(vis_hbm, inputs[0], r["in_sem"].at[0])]
    loads += [
        pltpu.make_async_copy(vel_hbm.at[:, c], inputs[1 + c], r["in_sem"].at[1 + c])
        for c in range(3)
    ]
    for load in loads:
        load.start()
    barrier = pltpu.get_barrier_semaphore()

    def greet(t, carry):
        pl.semaphore_signal(
            barrier, inc=1, device_id=(grp, lax.rem(dev + t, n_dev)), device_id_type=MESH
        )
        return carry

    lax.fori_loop(1, n_dev, greet, 0)
    for k in hops:
        pl.semaphore_signal(barrier, inc=1, device_id=stream_device(k), device_id_type=MESH)

    def transpose_field(f):
        for t in range(8):
            lanes = pl.ds(t * LANES, LANES)
            turned = jnp.concatenate([inputs[f][b, :, lanes] for b in LANE_SLOTS], axis=0).T
            for jj in range(4):
                stages[f][pl.ds(4 * t + jj, SIDE, stride=SIDE), :] = turned[
                    SIDE * jj : SIDE * jj + SIDE
                ]

    def spread(f):
        def send(t, carry):
            to = lax.rem(dev + t, n_dev)
            pltpu.make_async_remote_copy(
                src_ref=stages[f].at[pl.ds(multiple(to * rows, rows), rows)],
                dst_ref=mids[f].at[dev],
                send_sem=r["send_1"].at[f],
                recv_sem=r["recv_1"].at[f],
                device_id=(grp, to),
                device_id_type=MESH,
            ).start()
            return carry

        pltpu.make_async_copy(
            stages[f].at[pl.ds(multiple(dev * rows, rows), rows)], mids[f].at[dev],
            r["recv_1"].at[f],
        ).start()
        lax.fori_loop(1, n_dev, send, 0)

    group_of_lane = lax.broadcasted_iota(jnp.int32, (rows, LANES), 1) // SIDE

    def collect(f):
        pltpu.make_async_copy(mids[f], mids[f], r["recv_1"].at[f]).wait()
        mine = grids[f].at[pl.ds(H0 + dev * each, each), pl.ds(TOP, SIDE)]

        def assemble(to):
            base = (grp * n_dev + to) * 4
            made = None
            for place, slot in enumerate(LANE_SLOTS):
                old = lax.rem(source_ref[base + slot] // 4, n_dev)
                piece = mids[f][old]
                made = piece if made is None else jnp.where(group_of_lane == place, piece, made)
            asms[f][to] = made.reshape(each, SIDE, LANES)

        def send(t, carry):
            to = lax.rem(dev + t, n_dev)
            assemble(to)
            pltpu.make_async_remote_copy(
                src_ref=asms[f].at[to],
                dst_ref=mine,
                send_sem=r["send_2"].at[f],
                recv_sem=r["recv_2"].at[f],
                device_id=(grp, to),
                device_id_type=MESH,
            ).start()
            return carry

        lax.fori_loop(1, n_dev, send, 0)
        assemble(dev)
        pltpu.make_async_copy(asms[f].at[dev], mine, r["recv_2"].at[f]).start()

    def exchange(k, src, dst, send, recv):
        return pltpu.make_async_remote_copy(
            src_ref=src, dst_ref=dst, send_sem=send, recv_sem=recv,
            device_id=stream_device(k), device_id_type=MESH,
        )

    def start(copies):
        for copy in copies:
            copy.start()
        return copies

    def wait(copies):
        for copy in copies:
            copy.wait()

    def halos(x, own, halo, send, recv, *more):
        def part(lo):
            return x.at[(pl.ds(lo, halo), *more)]

        return [
            exchange(-1, part(halo), part(halo + own), send.at[0], recv.at[0]),
            exchange(1, part(own), part(0), send.at[1], recv.at[1]),
        ]

    def grid_halos(f):
        own = grids[f].at[pl.ds(H0, N0), pl.ds(TOP, SIDE)]
        pltpu.make_async_copy(own, own, r["recv_2"].at[f]).wait()
        body = pl.ds(TOP, SIDE)
        return start(halos(grids[f], N0, H0, r["send_h"].at[f], r["recv_h"].at[f], body))

    def grid_ready(f, copies):
        wait(copies)
        for edge, lo in ((0, 0), (count - 1, H0 + N0)):
            @pl.when(at == edge)
            def _():
                grids[f][pl.ds(lo, H0)] = jnp.zeros((H0, TALL, LANES), F32)

        def ghosts(ns):
            made = [(n, grids[f][n, BODY]) for n in ns]
            for n, v in made:
                grids[f][n, :TOP] = pltpu.roll(v[SIDE - TOP :], LANES // 2, 1)
                grids[f][n, TOP + SIDE :] = pltpu.roll(v[:TOP], LANES // 2, 1)

        steps(0, N0 + 2 * H0, 20, ghosts)

    def inside_of(own, halo):
        def inside(n):
            cell = at * own + n - halo
            return (cell >= 0) & (cell < count * own)

        return inside

    in0, in1 = inside_of(N0, H0), inside_of(N1, H1)
    in2, in3 = inside_of(N2, H2), inside_of(N3, H3)
    fine = Fine(SIDE, 2 * SIDE, 2 * SIDE, 1)
    lev1, lev2, lev3 = (Level(8, SIDE, SIDE, d) for d in (1, 2, 4))
    lane_f = lax.broadcasted_iota(jnp.int32, (LANES, LANES), 0)
    lane_c = lax.broadcasted_iota(jnp.int32, (LANES, LANES), 1)
    target = (lane_f // 64) * 64 + lax.rem(lane_f, 64) // 2
    down_m = [jnp.where(lane_c == target + 32 * jh, 0.5, 0.0).astype(F32) for jh in (0, 1)]
    target_t = (lane_c // 64) * 64 + lax.rem(lane_c, 64) // 2
    up_m = [jnp.where(lane_f == target_t + 32 * jh, 1.0, 0.0).astype(F32) for jh in (0, 1)]
    row8 = lax.broadcasted_iota(jnp.int32, (8, LANES), 0)
    lane8 = lax.broadcasted_iota(jnp.int32, (8, LANES), 1)
    tmp, half = r["tmp"], r["half"]

    def rows_halved(f, ms, totals):
        for i, total in enumerate(totals):
            tmp[i] = total
        made = [
            0.25 * (tmp[i, pl.ds(0, 16, stride=2), :] + tmp[i, pl.ds(1, 16, stride=2), :])
            for i in range(len(totals))
        ]
        for m, pairs in zip(ms, made):
            half[f, 0, m] = pairs[:8]
            half[f, 1, m] = pairs[8:]

    def lanes_halved(f):
        made = None
        for jh in (0, 1):
            part = jnp.dot(
                half[f, jh, :N1].reshape(N1 * 8, LANES), down_m[jh],
                precision=HIGHEST, preferred_element_type=F32,
            )
            made = part if made is None else made + part
        return made.reshape(N1, 8, LANES)

    def nu_pairs(ms):
        rows_halved(
            3, ms, [grids[0][H0 + 2 * m, BODY] + grids[0][H0 + 2 * m + 1, BODY] for m in ms]
        )

    def down_0(c):
        grid, s, a, b = grids[1 + c], r[f"s0{c}"], r[f"a0{c}"], r[f"b0{c}"]

        def first(ns):
            made = []
            for n in ns:
                g = [r["g0"][i, n] for i in range(6)]
                v = grid[n, BODY]
                scaled = r["w0"][n] * v
                made.append(
                    (n, scaled,
                     (1.0 - RELAX) * v + (scaled + gathered(fine, g, grid, BODY, n, v)))
                )
            for n, scaled, v in made:
                s[n] = scaled
                put(a, n, v)

        steps(1, N0 + 2 * H0 - 1, 19, first)
        sweep(
            fine, 2, N0 + 2 * H0 - 2, 18, r["g0"], [s], [a], lambda _, n, v: put(b, n, v), BODY
        )

        def pairs(ms):
            totals = []
            for m in ms:
                n = H0 + 2 * m
                [one] = residual(fine, n, r["g0"], r["iw0"], [s], [b], BODY)
                [two] = residual(fine, n + 1, r["g0"], r["iw0"], [s], [b], BODY)
                totals.append(one + two)
            rows_halved(c, ms, totals)

        steps(0, N1, 8, pairs)
        r["x1"][pl.ds(H1, N1), c] = lanes_halved(c)

    def blank(x, inside, ranges):
        for lo, hi in ranges:
            def planes(ns):
                made = [(n, jnp.where(inside(n), x[n], 0.0)) for n in ns]
                for n, v in made:
                    x[n] = v

            steps(lo, hi, 12, planes)

    def scaled(x, w, outs, lo, hi):
        def planes(ns):
            made = [(n, c, w[n] * x[n, c]) for n in ns for c in range(3)]
            for n, c, v in made:
                outs[c][n] = v

        steps(lo, hi, ANY, planes)

    nu1, nu2, nu3 = r["nu1"], r["nu2"], r["nu3"]

    def nu_down(fine_nu, coarse_nu, halo_f, halo_c, d):
        def planes(ms):
            made = [
                (m, 0.125 * pair_sum(fine_nu[halo_f + 2 * m] + fine_nu[halo_f + 2 * m + 1], d))
                for m in ms
            ]
            for m, v in made:
                coarse_nu[halo_c + m] = v

        return planes

    def staged(f):
        loads[f].wait()
        transpose_field(f)

    staged(0)
    pl.semaphore_wait(barrier, n_dev - 1 + len(hops))
    spread(0)
    staged(1)
    spread(1)
    staged(2)
    collect(0)
    spread(2)
    staged(3)
    moving = grid_halos(0)
    collect(1)
    spread(3)

    grid_ready(0, moving)
    steps(0, N1, 8, nu_pairs)
    nu1[pl.ds(H1, N1)] = lanes_halved(3)
    moving = start(halos(nu1, N1, H1, r["send_e"].at[0], r["recv_e"].at[0]))
    weights(
        fine, DIFFUSION_NUMBER, 1, N0 + 2 * H0 - 1, 10, grids[0], BODY, in0, r["g0"], r["w0"],
        r["iw0"],
    )
    collect(2)
    waiting = grid_halos(1)
    wait(moving)
    blank(nu1, in1, [(0, H1), (H1 + N1, N1 + 2 * H1)])
    steps(0, N2, 8, nu_down(nu1, nu2, H1, H2, 1))
    moving = start(halos(nu2, N2, H2, r["send_e"].at[1], r["recv_e"].at[1]))
    collect(3)
    weights(
        lev1, DIFFUSION_NUMBER / 4, 1, N1 + 2 * H1 - 1, ANY, nu1, ALL, in1, r["g1"], r["w1"], r["iw1"]
    )
    wait(moving)
    blank(nu2, in2, [(0, H2), (H2 + N2, N2 + 2 * H2)])
    steps(0, N3, 8, nu_down(nu2, nu3, H2, H3, 2))
    moving = start(
        [
            exchange(
                k, nu3.at[pl.ds(H3, N3)], nu3.at[pl.ds(H3 - k * N3, N3)],
                r["send_n3"].at[i], r["recv_n3"].at[i],
            )
            for i, k in enumerate(hops)
        ]
    )
    weights(
        lev2, DIFFUSION_NUMBER / 16, 1, N2 + 2 * H2 - 1, ANY, nu2, ALL, in2, r["g2"], r["w2"],
        r["iw2"],
    )
    grid_ready(1, waiting)
    waiting = grid_halos(2)
    down_0(0)
    wait(moving)
    blank(nu3, in3, [(0, H3), (H3 + N3, N3 + 2 * H3)])
    planes3 = N3 + 2 * H3
    lo = H3 - 2 - (BOTTOM - 1)
    weights(
        lev3, DIFFUSION_NUMBER / 64, lo, planes3 - lo, ANY, nu3, ALL, in3, r["g3"], r["w3"], r["iw3"]
    )
    grid_ready(2, waiting)
    waiting = grid_halos(3)
    down_0(1)
    grid_ready(3, waiting)
    down_0(2)

    x1, x2, x3 = r["x1"], r["x2"], r["x3"]
    s1, a1, b1 = three("s", 1), three("a", 1), three("b", 1)
    s2, a2, b2 = three("s", 2), three("a", 2), three("b", 2)
    s3, a3, b3 = three("s", 3), three("a", 3), three("b", 3)
    wait(start(halos(x1, N1, H1, r["send_e"].at[2], r["recv_e"].at[2])))
    blank(x1, in1, [(0, H1), (H1 + N1, N1 + 2 * H1)])
    scaled(x1, r["w1"], s1, 1, N1 + 2 * H1 - 1)
    sweep(lev1, 2, N1 + 2 * H1 - 2, ANY, r["g1"], s1, s1, storing(a1))

    def down(level, ms, halo_f, halo_c, g, iw, s, a, x, d):
        made = []
        for m in ms:
            n = halo_f + 2 * m
            one = residual(level, n, g, iw, s, a)
            two = residual(level, n + 1, g, iw, s, a)
            for c in range(3):
                made.append((m, c, 0.125 * pair_sum(one[c] + two[c], d)))
        for m, c, v in made:
            x[halo_c + m, c] = v

    steps(0, N2, ANY, lambda ms: down(lev1, ms, H1, H2, r["g1"], r["iw1"], s1, a1, x2, 1))

    place2 = lax.rem(row8, 2) * 2 + lax.rem(lane8, 2)
    pk2, pk3 = r["pk2"], r["pk3"]

    def pack_2(ms):
        made = []
        for m in ms:
            one = x2[H2 + m, 0]
            for c in (1, 2):
                one = jnp.where(place2 == c, x2[H2 + m, c], one)
            made.append((m, one))
        for m, one in made:
            pk2[H2 + m] = one

    steps(0, N2, 8, pack_2)
    wait(start(halos(pk2, N2, H2, r["send_e"].at[3], r["recv_e"].at[3])))

    def unpack_2(ns):
        made = []
        for n in ns:
            packed = jnp.where(in2(n), pk2[n], 0.0)
            for c in range(3):
                made.append((n, c, pair_sum(jnp.where(place2 == c, packed, 0.0), 1)))
        for n, c, v in made:
            x2[n, c] = v

    steps(0, H2, 6, unpack_2)
    steps(H2 + N2, N2 + 2 * H2, 6, unpack_2)
    scaled(x2, r["w2"], s2, 1, N2 + 2 * H2 - 1)
    sweep(lev2, 2, N2 + 2 * H2 - 2, ANY, r["g2"], s2, s2, storing(a2))
    steps(0, N3, 4, lambda ms: down(lev2, ms, H2, H3, r["g2"], r["iw2"], s2, a2, x3, 2))

    row_of, lane_of = lax.rem(row8, 4), lax.rem(lane8, 4)
    made = None
    for m in range(N3):
        line = x3[H3 + m, 0]
        for c in (1, 2):
            line = jnp.where(lane_of == c, x3[H3 + m, c], line)
        made = line if made is None else jnp.where(row_of == m, line, made)
    pk3[REACH] = made
    wait(
        start(
            [
                exchange(k, pk3.at[REACH], pk3.at[REACH - k], r["send_r3"].at[i], r["recv_r3"].at[i])
                for i, k in enumerate(hops)
            ]
        )
    )

    def unpack_3(bs):
        made = []
        for b in bs:
            packed = pk3[b]
            for m in range(N3):
                n = N3 * b + m
                line = jnp.where((row_of == m) & in3(n), packed, 0.0)
                line = spread_rows(spread_rows(line, 1), 2)
                for c in range(3):
                    one = jnp.where(lane_of == c, line, 0.0)
                    made.append((n, c, spread_lanes(spread_lanes(one, 1), 2)))
        for n, c, v in made:
            x3[n, c] = v

    steps(0, REACH, ANY, unpack_3)
    steps(REACH + 1, 2 * REACH + 1, ANY, unpack_3)
    scaled(x3, r["w3"], s3, lo, planes3 - lo)
    src = s3
    for turn in range(1, BOTTOM):
        dst = a3 if turn % 2 else b3
        sweep(
            lev3, lo + turn, planes3 - lo - turn, ANY, r["g3"], s3, src, storing(dst)
        )
        src = dst

    def add(bs, coarse, start_f, start_c):
        def pairs(ms):
            made = []
            for m in ms:
                for c in range(3):
                    more = coarse[c][start_c + m]
                    for twin in (0, 1):
                        n = start_f + 2 * m + twin
                        made.append((c, n, bs[c][n] + more))
            for c, n, v in made:
                bs[c][n] = v

        return pairs

    steps(0, (N2 + 8) // 2, ANY, add(a2, src, H2 - 4, H3 - 2))
    sweep(lev2, 3, N2 + 2 * H2 - 3, ANY, r["g2"], s2, a2, storing(b2))
    sweep(lev2, 4, N2 + 2 * H2 - 4, ANY, r["g2"], s2, b2, storing(a2))
    steps(0, (N1 + 8) // 2, ANY, add(a1, a2, H1 - 4, H2 - 2))
    sweep(lev1, 3, N1 + 2 * H1 - 3, ANY, r["g1"], s1, a1, storing(b1))
    sweep(lev1, 4, N1 + 2 * H1 - 4, ANY, r["g1"], s1, b1, storing(a1))

    wide = N1 + 2
    outs = (o_0, o_1, o_2)
    for c in range(3):
        coarse = a1[c][pl.ds(H1 - 1, wide)].reshape(wide * 8, LANES)
        for jh in (0, 1):
            half[c, jh] = jnp.dot(
                coarse, up_m[jh], precision=HIGHEST, preferred_element_type=F32
            ).reshape(wide, 8, LANES)

    for c in range(3):
        s, a, b = r[f"s0{c}"], r[f"a0{c}"], r[f"b0{c}"]

        def refined(ms, c=c, b=b):
            for i, m in enumerate(ms):
                for jh in (0, 1):
                    for twin in (0, 1):
                        tmp[i, pl.ds(16 * jh + twin, 8, stride=2), :] = half[c, jh, m]
            made = []
            for i, m in enumerate(ms):
                for twin in (0, 1):
                    n = H0 - 2 + 2 * m + twin
                    made.append((n, b[n, BODY] + tmp[i]))
            for n, v in made:
                put(b, n, v)

        steps(0, wide, 9, refined)
    s0, a0, b0 = three("s", 0), three("a", 0), three("b", 0)

    def to_a0(c, _, n, v):
        put(a0[c], n, v)

    def to_out(c, _, n, v):
        outs[c][n - H0] = v

    for c in range(3):
        sweep(
            fine, 3, N0 + 2 * H0 - 3, 17, r["g0"], [s0[c]], [b0[c]],
            functools.partial(to_a0, c), BODY,
        )
        sweep(
            fine, 4, N0 + 2 * H0 - 4, 16, r["g0"], [s0[c]], [a0[c]],
            functools.partial(to_out, c), BODY,
        )

    for f in range(4):
        most = stages[f].at[pl.ds(0, (n_dev - 1) * rows)]
        pltpu.make_async_copy(most, most, r["send_1"].at[f]).wait()
        most = asms[f].at[pl.ds(0, n_dev - 1)]
        pltpu.make_async_copy(most, most, r["send_2"].at[f]).wait()


def whole(n_dev, source, velocity_old, viscosity_old):
    vmem = pl.BlockSpec(memory_space=pltpu.VMEM)
    anywhere = pl.BlockSpec(memory_space=pl.ANY)
    named = names_of_scratch(n_dev)
    return pl.pallas_call(
        functools.partial(whole_kernel, tuple(named)),
        out_shape=[jax.ShapeDtypeStruct((N0, SIDE, LANES), F32)] * 3,
        in_specs=[pl.BlockSpec(memory_space=pltpu.SMEM), anywhere, anywhere],
        out_specs=[vmem] * 3,
        scratch_shapes=list(named.values()),
        compiler_params=pltpu.CompilerParams(
            collective_id=0, has_side_effects=True, vmem_limit_bytes=VMEM_LIMIT
        ),
        name="whole",
    )(source, velocity_old, viscosity_old)


def blocks_kernel(e_0, e_1, e_2, out_ref):
    for c, e in enumerate((e_0, e_1, e_2)):
        for t in range(8):
            parts = [e[pl.ds(4 * t + jj, SIDE, stride=SIDE), :] for jj in range(4)]
            turned = jnp.concatenate(parts, axis=0).T
            for at, slot in enumerate(LANE_SLOTS):
                out_ref[slot, c, :, pl.ds(t * LANES, LANES)] = turned[SIDE * at : SIDE * at + SIDE]


def to_blocks(planes):
    vmem = pl.BlockSpec(memory_space=pltpu.VMEM)
    return pl.pallas_call(
        blocks_kernel,
        out_shape=jax.ShapeDtypeStruct((4, 3, SIDE, SIDE * SIDE), F32),
        in_specs=[vmem] * 3,
        out_specs=vmem,
        compiler_params=pltpu.CompilerParams(vmem_limit_bytes=VMEM_LIMIT),
        name="to_blocks",
    )(*[p.reshape(SIDE * SIDE, LANES) for p in planes])


def solution(mesh):
    n_dev = mesh.shape["dev"]

    def local(velocity_old, viscosity_old, source):
        return to_blocks(whole(n_dev, source, velocity_old, viscosity_old))

    return jax.shard_map(
        local,
        mesh=mesh,
        in_specs=(P(("grp", "dev"), None, None, None), P(("grp", "dev"), None, None), P()),
        out_specs=P(("grp", "dev"), None, None, None),
        check_vma=False,
    )
```

```python
import functools

import jax
import jax.numpy as jnp
from jax import lax
from jax.experimental import pallas as pl
from jax.experimental.pallas import tpu as pltpu
from jax.sharding import PartitionSpec as P

F32 = jnp.float32
SIDE = 32
LANES = 128
DIFFUSION_NUMBER = 1000.0
RELAX = 0.8
BOTTOM = 8
LANE_SLOTS = (0, 2, 1, 3)
ANY = 64
H0, H1 = 4, 5
N0, N1, N2, N3 = 32, 16, 8, 4
REACH = 3
H2, H3 = REACH * N2, REACH * N3
VMEM_LIMIT = 48 * 1024 * 1024
MESH = pl.DeviceIdType.MESH
HIGHEST = lax.Precision.HIGHEST


def positions():
    grp, dev = lax.axis_index("grp"), lax.axis_index("dev")
    n_grp, n_dev = lax.axis_size("grp"), lax.axis_size("dev")
    return grp, dev, n_grp, n_dev


def stream_device(offset):
    grp, dev, n_grp, n_dev = positions()
    at = lax.rem(grp * n_dev + dev + offset + n_grp * n_dev, n_grp * n_dev)
    return (at // n_dev, lax.rem(at, n_dev))


STRIDE_TILES = 8
TOP = 8
TALL = SIDE + 2 * TOP
BODY = slice(TOP, TOP + SIDE)


def multiple(value, of):
    return pl.multiple_of(value, of)


def put(ref, n, v):
    ref[n, BODY] = v
    ref[n, :TOP] = pltpu.roll(v[SIDE - TOP :], LANES // 2, 1)
    ref[n, TOP + SIDE :] = pltpu.roll(v[:TOP], LANES // 2, 1)


def fine_beside(ref, n, v):
    return (
        pltpu.roll(v, 1, 1),
        pltpu.roll(v, LANES - 1, 1),
        ref[n, TOP - 1 : TOP + SIDE - 1],
        ref[n, TOP + 1 : TOP + SIDE + 1],
    )


def steps(lo, hi, most, body):
    count = hi - lo
    size = -(-count // -(-count // most))
    full, rest = divmod(count, size)

    def step(i, carry):
        body([lo + size * i + t for t in range(size)])
        return carry

    if full == 1:
        body(list(range(lo, lo + size)))
    else:
        lax.fori_loop(0, full, step, 0)
    if rest:
        body(list(range(hi - rest, hi)))


class Level:
    def __init__(self, rows, wide, high, d):
        self.wide, self.d = wide, d
        row = lax.broadcasted_iota(jnp.int32, (rows, LANES), 0)
        lane = lax.broadcasted_iota(jnp.int32, (rows, LANES), 1)
        deep = lax.rem(lane, high)
        self.ok_zm = deep >= d
        self.ok_zp = deep < high - d
        self.ok_ym = (row >= d) | (lane >= wide)
        self.ok_yp = (row < rows - d) | (lane < LANES - wide)
        self.wrap_m = row < d
        self.wrap_p = row >= rows - d

    def beside(self, ref, n, a):
        wide, d = self.wide, self.d
        zm = pltpu.roll(a, d, 1)
        zp = pltpu.roll(a, LANES - d, 1)
        ym = pltpu.roll(a, d, 0)
        ym = jnp.where(self.wrap_m, pltpu.roll(ym, wide, 1), ym)
        yp = pltpu.roll(a, 8 - d, 0)
        yp = jnp.where(self.wrap_p, pltpu.roll(yp, LANES - wide, 1), yp)
        return zm, zp, ym, yp


class Fine(Level):
    def beside(self, ref, n, a):
        return fine_beside(ref, n, a)


def spread_rows(a, d):
    row = lax.broadcasted_iota(jnp.int32, a.shape, 0)
    first = lax.rem(row // d, 2) == 0
    return a + jnp.where(first, pltpu.roll(a, a.shape[0] - d, 0), pltpu.roll(a, d, 0))


def spread_lanes(a, d):
    lane = lax.broadcasted_iota(jnp.int32, a.shape, 1)
    first = lax.rem(lane // d, 2) == 0
    return a + jnp.where(first, pltpu.roll(a, LANES - d, 1), pltpu.roll(a, d, 1))


def pair_sum(a, d):
    return spread_lanes(spread_rows(a, d), d)


def weights(level, coef, lo, hi, most, nu_ref, at, inside, g_ref, w_ref, iw_ref):
    def planes(ns):
        made = []
        for n in ns:
            nu = nu_ref[n, at]
            xm, xp = nu_ref[n - 1, at], nu_ref[n + 1, at]
            zm, zp, ym, yp = level.beside(nu_ref, n, nu)
            zm = jnp.where(level.ok_zm, zm, 0.0)
            zp = jnp.where(level.ok_zp, zp, 0.0)
            ym = jnp.where(level.ok_ym, ym, 0.0)
            yp = jnp.where(level.ok_yp, yp, 0.0)
            total = 6.0 * nu + ((xm + xp) + (zm + zp) + (ym + yp))
            diag = 1.0 + (0.5 * coef) * total
            w = RELAX / diag
            k = w * jnp.where(inside(n), 0.5 * coef, 0.0)
            made.append(
                (
                    n, w, diag * (1.0 / RELAX), k * (nu + xm), k * (nu + xp),
                    jnp.where(level.ok_zm, k * (nu + zm), 0.0),
                    jnp.where(level.ok_zp, k * (nu + zp), 0.0),
                    jnp.where(level.ok_ym, k * (nu + ym), 0.0),
                    jnp.where(level.ok_yp, k * (nu + yp), 0.0),
                )
            )
        for n, w, iw, *g in made:
            w_ref[n] = w
            iw_ref[n] = iw
            for i in range(6):
                g_ref[i, n] = g[i]

    steps(lo, hi, most, planes)


def gathered(level, g, src, at, n, v):
    zm, zp, ym, yp = level.beside(src, n, v)
    return (
        (g[0] * src[n - 1, at] + g[1] * src[n + 1, at])
        + (g[2] * zm + g[3] * zp)
        + (g[4] * ym + g[5] * yp)
    )


ALL = slice(None)


def sweep(level, lo, hi, most, g_ref, s_refs, srcs, store, at=ALL):
    def planes(ns):
        made = []
        for n in ns:
            g = [g_ref[i, n] for i in range(6)]
            for c, (s, src) in enumerate(zip(s_refs, srcs)):
                v = src[n, at]
                made.append(
                    (c, n, (1.0 - RELAX) * v + (s[n] + gathered(level, g, src, at, n, v)))
                )
        for c, n, v in made:
            store(c, n, v)

    steps(lo, hi, most, planes)


def storing(refs):
    def store(c, n, v):
        refs[c][n] = v

    return store


def residual(level, n, g_ref, iw_ref, s_refs, srcs, at=ALL):
    g = [g_ref[i, n] for i in range(6)]
    made = []
    for s, src in zip(s_refs, srcs):
        v = src[n, at]
        made.append(iw_ref[n] * ((s[n] + gathered(level, g, src, at, n, v)) - RELAX * v))
    return made


def names_of_scratch(n_dev):
    n0, n1, n2, n3 = N0 + 2 * H0, N1 + 2 * H1, N2 + 2 * H2, N3 + 2 * H3

    def vmem(*shape):
        return pltpu.VMEM((*shape, LANES), F32)

    def dma(*shape):
        return pltpu.SemaphoreType.DMA(shape)

    named = {"vis": pltpu.VMEM((4, SIDE, SIDE * SIDE), F32)}
    for c in range(3):
        named[f"vel{c}"] = pltpu.VMEM((4, SIDE, SIDE * SIDE), F32)
    for f in range(4):
        named[f"stage{f}"] = vmem(SIDE * SIDE)
        named[f"mid{f}"] = vmem(n_dev, STRIDE_TILES, 8)
        named[f"asm{f}"] = vmem(n_dev + 2, STRIDE_TILES + 2, 8)
        named[f"grid{f}"] = vmem(n0, TALL)
    named |= {"g0": vmem(6, n0, SIDE), "w0": vmem(n0, SIDE), "iw0": vmem(n0, SIDE)}
    for c in range(3):
        named[f"s0{c}"] = vmem(n0, SIDE)
        named[f"a0{c}"] = vmem(n0, TALL)
        named[f"b0{c}"] = vmem(n0, TALL)
    named |= {"tmp": vmem(9, SIDE), "half": vmem(4, 2, N1 + 2, 8)}
    for level, n in ((1, n1), (2, n2), (3, n3)):
        named |= {
            f"nu{level}": vmem(n, 8), f"g{level}": vmem(6, n, 8),
            f"w{level}": vmem(n, 8), f"iw{level}": vmem(n, 8),
        }
        for c in range(3):
            for kind in "xsab":
                named[f"{kind}{level}{c}"] = vmem(n, 8)
    for f in range(4):
        named[f"pack{f}"] = vmem(2 * REACH + 1, 2, 8)
    named |= {
        "in_sem": dma(4),
        "send_1": dma(4), "recv_1": dma(4), "send_2": dma(4), "recv_2": dma(4),
        "send_e": dma(4, 2), "recv_e": dma(4, 2),
        "send_p": dma(4, 2 * REACH), "recv_p": dma(4, 2 * REACH),
    }
    return named


def whole_kernel(names, source_ref, vel_hbm, vis_hbm, o_0, o_1, o_2, *scratch):
    r = dict(zip(names, scratch))
    grp, dev, n_grp, n_dev = positions()
    at = grp * n_dev + dev
    count = n_grp * n_dev
    phase, rg = dev // 4, lax.rem(dev, 4)
    hops = [k for k in range(-REACH, REACH + 1) if k]
    stages, mids = [r[f"stage{f}"] for f in range(4)], [r[f"mid{f}"] for f in range(4)]
    asms, grids = [r[f"asm{f}"] for f in range(4)], [r[f"grid{f}"] for f in range(4)]
    inputs = [r["vis"]] + [r[f"vel{c}"] for c in range(3)]

    loads = [pltpu.make_async_copy(vis_hbm, inputs[0], r["in_sem"].at[0])]
    loads += [
        pltpu.make_async_copy(vel_hbm.at[:, c], inputs[1 + c], r["in_sem"].at[1 + c])
        for c in range(3)
    ]
    for load in loads:
        load.start()
    barrier = pltpu.get_barrier_semaphore()

    def greet(t, carry):
        pl.semaphore_signal(
            barrier, inc=1, device_id=(grp, lax.rem(dev + t, n_dev)), device_id_type=MESH
        )
        return carry

    lax.fori_loop(1, n_dev, greet, 0)
    next_first = (lax.rem(grp + 1, n_grp), 0)
    before_last = (lax.rem(grp + n_grp - 1, n_grp), n_dev - 1)
    for beside in (next_first, before_last):
        pl.semaphore_signal(barrier, inc=1, device_id=beside, device_id_type=MESH)

    @pl.when(dev == 0)
    def _():
        def back(t, carry):
            pl.semaphore_signal(
                barrier, inc=1, device_id=(before_last[0], t), device_id_type=MESH
            )
            return carry

        lax.fori_loop(0, n_dev, back, 0)

    @pl.when(dev == n_dev - 1)
    def _():
        def onward(t, carry):
            pl.semaphore_signal(barrier, inc=1, device_id=(next_first[0], t), device_id_type=MESH)
            return carry

        lax.fori_loop(0, n_dev, onward, 0)

    for k in hops:
        pl.semaphore_signal(barrier, inc=1, device_id=stream_device(k), device_id_type=MESH)

    def transpose_field(f):
        for t in range(8):
            lanes = pl.ds(t * LANES, LANES)
            turned = jnp.concatenate([inputs[f][b, :, lanes] for b in LANE_SLOTS], axis=0).T
            for jj in range(4):
                stages[f][pl.ds(4 * t + jj, SIDE, stride=SIDE), :] = turned[
                    SIDE * jj : SIDE * jj + SIDE
                ]

    def spread(f):
        tiles = stages[f].reshape(STRIDE_TILES, 4, 4, 8, LANES)

        def send(t, carry):
            to = lax.rem(dev + t, n_dev)
            pltpu.make_async_remote_copy(
                src_ref=tiles.at[:, to // 4, lax.rem(to, 4)],
                dst_ref=mids[f].at[dev],
                send_sem=r["send_1"].at[f],
                recv_sem=r["recv_1"].at[f],
                device_id=(grp, to),
                device_id_type=MESH,
            ).start()
            return carry

        pltpu.make_async_copy(tiles.at[:, phase, rg], mids[f].at[dev], r["recv_1"].at[f]).start()
        lax.fori_loop(1, n_dev, send, 0)

    group_of_lane = lax.broadcasted_iota(jnp.int32, (STRIDE_TILES, 8, LANES), 2) // SIDE
    far = STRIDE_TILES + 1

    def collect(f):
        pltpu.make_async_copy(mids[f], mids[f], r["recv_1"].at[f]).wait()
        grid = grids[f].reshape(STRIDE_TILES + 2, 4, TALL, LANES)
        asm = asms[f]

        def assemble(d, carry):
            base = (grp * n_dev + d) * 4
            made = None
            for place, slot in enumerate(LANE_SLOTS):
                old = lax.rem(source_ref[base + slot] // 4, n_dev)
                piece = mids[f][old]
                made = piece if made is None else jnp.where(group_of_lane == place, piece, made)
            asm[d + 1, 1:far] = made
            asm[d + 2, 0] = made[STRIDE_TILES - 1]
            asm[d, far] = made[0]
            return carry

        for d in range(n_dev):
            assemble(d, 0)

        def parts(d, lo, hi):
            places = pl.ds(lo, hi - lo)
            return (
                asm.at[d + 1, places],
                grid.at[places, phase, pl.ds(multiple(TOP + 8 * rg, 8), 8)],
            )

        def remote(d, lo, hi, target):
            src, dst = parts(d, lo, hi)
            pltpu.make_async_remote_copy(
                src_ref=src, dst_ref=dst, send_sem=r["send_2"].at[f], recv_sem=r["recv_2"].at[f],
                device_id=target, device_id_type=MESH,
            ).start()

        def local(d, lo, hi, target):
            src, dst = parts(d, lo, hi)
            pltpu.make_async_copy(src, dst, r["recv_2"].at[f]).start()

        def to_device(copy, d):
            @pl.when(d == 0)
            def _():
                copy(d, 1, far + 1, (grp, d))

            @pl.when(d == n_dev - 1)
            def _():
                copy(d, 0, far, (grp, d))

            @pl.when((d > 0) & (d < n_dev - 1))
            def _():
                copy(d, 0, far + 1, (grp, d))

        def send(t, carry):
            to_device(remote, lax.rem(dev + t, n_dev))
            return carry

        lax.fori_loop(1, n_dev, send, 0)
        to_device(local, dev)
        remote(n_dev, 0, 1, next_first)
        remote(-1, far, far + 1, before_last)

    def exchange(k, src, dst, send, recv):
        return pltpu.make_async_remote_copy(
            src_ref=src, dst_ref=dst, send_sem=send, recv_sem=recv,
            device_id=stream_device(k), device_id_type=MESH,
        )

    def start(copies):
        for copy in copies:
            copy.start()
        return copies

    def wait(copies):
        for copy in copies:
            copy.wait()

    def halos(x, own, halo, send, recv, *more):
        def part(lo):
            return x.at[(pl.ds(lo, halo), *more)]

        return [
            exchange(-1, part(halo), part(halo + own), send.at[0], recv.at[0]),
            exchange(1, part(own), part(0), send.at[1], recv.at[1]),
        ]

    def grid_ready(f):
        body = grids[f].at[:, pl.ds(TOP, SIDE)]
        pltpu.make_async_copy(body, body, r["recv_2"].at[f]).wait()
        for edge, lo in ((0, 0), (count - 1, H0 + N0)):
            @pl.when(at == edge)
            def _():
                grids[f][pl.ds(lo, H0)] = jnp.zeros((H0, TALL, LANES), F32)

        def ghosts(ns):
            made = [(n, grids[f][n, BODY]) for n in ns]
            for n, v in made:
                grids[f][n, :TOP] = pltpu.roll(v[SIDE - TOP :], LANES // 2, 1)
                grids[f][n, TOP + SIDE :] = pltpu.roll(v[:TOP], LANES // 2, 1)

        steps(0, N0 + 2 * H0, 20, ghosts)

    def inside_of(own, halo):
        def inside(n):
            cell = at * own + n - halo
            return (cell >= 0) & (cell < count * own)

        return inside

    in0, in1 = inside_of(N0, H0), inside_of(N1, H1)
    in2, in3 = inside_of(N2, H2), inside_of(N3, H3)
    fine = Fine(SIDE, 2 * SIDE, 2 * SIDE, 1)
    lev1, lev2, lev3 = (Level(8, SIDE, SIDE, d) for d in (1, 2, 4))
    lane_f = lax.broadcasted_iota(jnp.int32, (LANES, LANES), 0)
    lane_c = lax.broadcasted_iota(jnp.int32, (LANES, LANES), 1)
    target = (lane_f // 64) * 64 + lax.rem(lane_f, 64) // 2
    down_m = [jnp.where(lane_c == target + 32 * jh, 0.5, 0.0).astype(F32) for jh in (0, 1)]
    target_t = (lane_c // 64) * 64 + lax.rem(lane_c, 64) // 2
    up_m = [jnp.where(lane_f == target_t + 32 * jh, 1.0, 0.0).astype(F32) for jh in (0, 1)]
    row8 = lax.broadcasted_iota(jnp.int32, (8, LANES), 0)
    lane8 = lax.broadcasted_iota(jnp.int32, (8, LANES), 1)
    tmp, half = r["tmp"], r["half"]

    def rows_halved(f, ms, totals):
        for i, total in enumerate(totals):
            tmp[i] = total
        made = [
            0.25 * (tmp[i, pl.ds(0, 16, stride=2), :] + tmp[i, pl.ds(1, 16, stride=2), :])
            for i in range(len(totals))
        ]
        for m, pairs in zip(ms, made):
            half[f, 0, m] = pairs[:8]
            half[f, 1, m] = pairs[8:]

    def lanes_halved(f):
        made = None
        for jh in (0, 1):
            part = jnp.dot(
                half[f, jh, :N1].reshape(N1 * 8, LANES), down_m[jh],
                precision=HIGHEST, preferred_element_type=F32,
            )
            made = part if made is None else made + part
        return made.reshape(N1, 8, LANES)

    def nu_pairs(ms):
        rows_halved(
            3, ms, [grids[0][H0 + 2 * m, BODY] + grids[0][H0 + 2 * m + 1, BODY] for m in ms]
        )

    def down_0(c):
        grid, s, a, b = grids[1 + c], r[f"s0{c}"], r[f"a0{c}"], r[f"b0{c}"]

        def first(ns):
            made = []
            for n in ns:
                g = [r["g0"][i, n] for i in range(6)]
                v = grid[n, BODY]
                scaled = r["w0"][n] * v
                made.append(
                    (n, scaled,
                     (1.0 - RELAX) * v + (scaled + gathered(fine, g, grid, BODY, n, v)))
                )
            for n, scaled, v in made:
                s[n] = scaled
                put(a, n, v)

        steps(1, N0 + 2 * H0 - 1, 19, first)
        sweep(
            fine, 2, N0 + 2 * H0 - 2, 18, r["g0"], [s], [a], lambda _, n, v: put(b, n, v), BODY
        )

        def pairs(ms):
            totals = []
            for m in ms:
                n = H0 + 2 * m
                [one] = residual(fine, n, r["g0"], r["iw0"], [s], [b], BODY)
                [two] = residual(fine, n + 1, r["g0"], r["iw0"], [s], [b], BODY)
                totals.append(one + two)
            rows_halved(c, ms, totals)

        steps(0, N1, 8, pairs)
        r[f"x1{c}"][pl.ds(H1, N1)] = lanes_halved(c)

    def blank(x, inside, ranges):
        for lo, hi in ranges:
            def planes(ns):
                made = [(n, jnp.where(inside(n), x[n], 0.0)) for n in ns]
                for n, v in made:
                    x[n] = v

            steps(lo, hi, 12, planes)

    def scaled(x, w, out, lo, hi):
        def planes(ns):
            made = [(n, w[n] * x[n]) for n in ns]
            for n, v in made:
                out[n] = v

        steps(lo, hi, ANY, planes)

    place = lax.rem(row8, 2) * 2 + lax.rem(lane8, 2)

    def pack(f, x):
        for h in range(N2 // 4):
            made = x[H2 + 4 * h]
            for p in range(1, 4):
                made = jnp.where(place == p, x[H2 + 4 * h + p], made)
            r[f"pack{f}"][REACH, h] = made
        packed = r[f"pack{f}"]
        return start(
            [
                exchange(
                    k, packed.at[REACH], packed.at[REACH - k],
                    r["send_p"].at[f, i], r["recv_p"].at[f, i],
                )
                for i, k in enumerate(hops)
            ]
        )

    def unpack(f, x, moving):
        wait(moving)

        def blocks(bs):
            made = []
            for b in bs:
                for h in range(N2 // 4):
                    packed = r[f"pack{f}"][b, h]
                    for p in range(4):
                        n = N2 * b + 4 * h + p
                        one = jnp.where((place == p) & in2(n), packed, 0.0)
                        made.append((n, pair_sum(one, 1)))
            for n, v in made:
                x[n] = v

        steps(0, REACH, ANY, blocks)
        steps(REACH + 1, 2 * REACH + 1, ANY, blocks)

    nu1, nu2, nu3 = r["nu1"], r["nu2"], r["nu3"]

    def nu_down(fine_nu, coarse_nu, halo_f, halo_c, d):
        def planes(ms):
            made = [
                (m, 0.125 * pair_sum(fine_nu[halo_f + 2 * m] + fine_nu[halo_f + 2 * m + 1], d))
                for m in ms
            ]
            for m, v in made:
                coarse_nu[halo_c + m] = v

        return planes

    def to_level_1(c):
        send, recv = r["send_e"].at[1 + c], r["recv_e"].at[1 + c]
        return start(halos(r[f"x1{c}"], N1, H1, send, recv))

    def staged(f):
        loads[f].wait()
        transpose_field(f)

    for f in range(4):
        staged(f)
    ends = jnp.where((dev == 0) | (dev == n_dev - 1), n_dev, 0)
    pl.semaphore_wait(barrier, n_dev - 1 + len(hops) + 2 + ends)
    spread(0)
    spread(1)
    collect(0)
    spread(2)
    collect(1)
    spread(3)
    collect(2)

    grid_ready(0)
    steps(0, N1, 8, nu_pairs)
    nu1[pl.ds(H1, N1)] = lanes_halved(3)
    moving = start(halos(nu1, N1, H1, r["send_e"].at[0], r["recv_e"].at[0]))
    collect(3)
    weights(
        fine, DIFFUSION_NUMBER, 1, N0 + 2 * H0 - 1, 10, grids[0], BODY, in0, r["g0"], r["w0"],
        r["iw0"],
    )
    wait(moving)
    blank(nu1, in1, [(0, H1), (H1 + N1, N1 + 2 * H1)])
    steps(0, N2, 8, nu_down(nu1, nu2, H1, H2, 1))
    moving = pack(3, nu2)
    weights(
        lev1, DIFFUSION_NUMBER / 4, 1, N1 + 2 * H1 - 1, ANY, nu1, ALL, in1, r["g1"], r["w1"], r["iw1"]
    )
    grid_ready(1)
    down_0(0)
    first = to_level_1(0)
    lo3 = H3 - 2 - (BOTTOM - 1)
    hi3 = N3 + 2 * H3 - lo3
    lo2, hi2 = 2 * lo3 - 2, 2 * hi3 + 2

    def down(level, ms, start_f, start_c, g, iw, s, a, x, d):
        made = []
        for m in ms:
            n = start_f + 2 * m
            [one] = residual(level, n, g, iw, [s], [a])
            [two] = residual(level, n + 1, g, iw, [s], [a])
            made.append((m, 0.125 * pair_sum(one + two, d)))
        for m, v in made:
            x[start_c + m] = v

    def to_level_2(c, moving):
        x, s, a = r[f"x1{c}"], r[f"s1{c}"], r[f"a1{c}"]
        wait(moving)
        blank(x, in1, [(0, H1), (H1 + N1, N1 + 2 * H1)])
        scaled(x, r["w1"], s, 1, N1 + 2 * H1 - 1)
        sweep(lev1, 2, N1 + 2 * H1 - 2, ANY, r["g1"], [s], [s], storing([a]))
        steps(
            0, N2, ANY,
            lambda ms: down(lev1, ms, H1, H2, r["g1"], r["iw1"], s, a, r[f"x2{c}"], 1),
        )
        return pack(c, r[f"x2{c}"])

    def add(b, coarse, start_f, start_c):
        def pairs(ms):
            made = []
            for m in ms:
                more = coarse[start_c + m]
                for twin in (0, 1):
                    n = start_f + 2 * m + twin
                    made.append((n, b[n] + more))
            for n, v in made:
                b[n] = v

        return pairs

    def bottom(c, moving):
        x, s, a, b = (r[f"{kind}2{c}"] for kind in "xsab")
        unpack(c, x, moving)
        scaled(x, r["w2"], s, lo2, hi2)
        sweep(lev2, lo2 + 1, hi2 - 1, ANY, r["g2"], [s], [s], storing([a]))
        x3, s3, a3, b3 = (r[f"{kind}3{c}"] for kind in "xsab")
        steps(
            lo3, hi3, ANY, lambda ms: down(lev2, ms, 0, 0, r["g2"], r["iw2"], s, a, x3, 2)
        )
        scaled(x3, r["w3"], s3, lo3, hi3)
        src = s3
        for turn in range(1, BOTTOM):
            dst = a3 if turn % 2 else b3
            sweep(lev3, lo3 + turn, hi3 - turn, ANY, r["g3"], [s3], [src], storing([dst]))
            src = dst
        steps(0, (N2 + 8) // 2, ANY, add(a, src, H2 - 4, H3 - 2))
        sweep(lev2, H2 - 3, H2 + N2 + 3, ANY, r["g2"], [s], [a], storing([b]))
        sweep(lev2, H2 - 2, H2 + N2 + 2, ANY, r["g2"], [s], [b], storing([a]))
        s1, a1, b1 = (r[f"{kind}1{c}"] for kind in "sab")
        steps(0, (N1 + 8) // 2, ANY, add(a1, a, H1 - 4, H2 - 2))
        sweep(lev1, 3, N1 + 2 * H1 - 3, ANY, r["g1"], [s1], [a1], storing([b1]))
        sweep(lev1, 4, N1 + 2 * H1 - 4, ANY, r["g1"], [s1], [b1], storing([a1]))

    outs = (o_0, o_1, o_2)

    def top(c):
        wide = N1 + 2
        coarse = r[f"a1{c}"][pl.ds(H1 - 1, wide)].reshape(wide * 8, LANES)
        for jh in (0, 1):
            half[c, jh] = jnp.dot(
                coarse, up_m[jh], precision=HIGHEST, preferred_element_type=F32
            ).reshape(wide, 8, LANES)
        s, a, b = r[f"s0{c}"], r[f"a0{c}"], r[f"b0{c}"]

        def refined(ms):
            for i, m in enumerate(ms):
                for jh in (0, 1):
                    for twin in (0, 1):
                        tmp[i, pl.ds(16 * jh + twin, 8, stride=2), :] = half[c, jh, m]
            made = []
            for i, m in enumerate(ms):
                for twin in (0, 1):
                    n = H0 - 2 + 2 * m + twin
                    made.append((n, b[n, BODY] + tmp[i]))
            for n, v in made:
                put(b, n, v)

        steps(0, wide, 9, refined)
        sweep(
            fine, 3, N0 + 2 * H0 - 3, 17, r["g0"], [s], [b], lambda _, n, v: put(a, n, v), BODY
        )

        def to_out(_, n, v):
            outs[c][n - H0] = v

        sweep(fine, 4, N0 + 2 * H0 - 4, 16, r["g0"], [s], [a], to_out, BODY)

    first = to_level_2(0, first)
    grid_ready(2)
    down_0(1)
    second = to_level_1(1)
    unpack(3, nu2, moving)
    steps(lo3 - 1, hi3 + 1, 12, nu_down(nu2, nu3, 0, 0, 2))
    weights(
        lev2, DIFFUSION_NUMBER / 16, lo2, hi2, 24, nu2, ALL, in2, r["g2"], r["w2"], r["iw2"]
    )
    weights(
        lev3, DIFFUSION_NUMBER / 64, lo3, hi3, ANY, nu3, ALL, in3, r["g3"], r["w3"], r["iw3"]
    )
    second = to_level_2(1, second)
    grid_ready(3)
    down_0(2)
    third = to_level_1(2)
    bottom(0, first)
    bottom(1, second)
    third = to_level_2(2, third)
    top(0)
    top(1)
    bottom(2, third)
    top(2)

    for f in range(4):
        most = mids[f].at[pl.ds(0, n_dev - 1)]
        pltpu.make_async_copy(most, most, r["send_1"].at[f]).wait()

        @pl.when((dev > 0) & (dev < n_dev - 1))
        def _():
            most = asms[f].at[pl.ds(0, n_dev - 1)]
            pltpu.make_async_copy(most, most, r["send_2"].at[f]).wait()

        @pl.when((dev == 0) | (dev == n_dev - 1))
        def _():
            most = stages[f].reshape(SIDE * SIDE // 8, 8, LANES).at[pl.ds(0, 128)]
            pltpu.make_async_copy(most, most, r["send_2"].at[f]).wait()
            rest = stages[f].reshape(SIDE * SIDE // 8, 8, LANES).at[pl.ds(0, 23)]
            pltpu.make_async_copy(rest, rest, r["send_2"].at[f]).wait()


def whole(n_dev, source, velocity_old, viscosity_old):
    vmem = pl.BlockSpec(memory_space=pltpu.VMEM)
    anywhere = pl.BlockSpec(memory_space=pltpu.HBM)
    named = names_of_scratch(n_dev)
    return pl.pallas_call(
        functools.partial(whole_kernel, tuple(named)),
        out_shape=[jax.ShapeDtypeStruct((N0, SIDE, LANES), F32)] * 3,
        in_specs=[pl.BlockSpec(memory_space=pltpu.SMEM), anywhere, anywhere],
        out_specs=[vmem] * 3,
        scratch_shapes=list(named.values()),
        compiler_params=pltpu.CompilerParams(
            collective_id=0, has_side_effects=True, vmem_limit_bytes=VMEM_LIMIT
        ),
        name="whole",
    )(source, velocity_old, viscosity_old)


def blocks_kernel(e_0, e_1, e_2, out_ref):
    for c, e in enumerate((e_0, e_1, e_2)):
        for t in range(8):
            parts = [e[pl.ds(4 * t + jj, SIDE, stride=SIDE), :] for jj in range(4)]
            turned = jnp.concatenate(parts, axis=0).T
            for at, slot in enumerate(LANE_SLOTS):
                out_ref[slot, c, :, pl.ds(t * LANES, LANES)] = turned[SIDE * at : SIDE * at + SIDE]


def to_blocks(planes):
    vmem = pl.BlockSpec(memory_space=pltpu.VMEM)
    return pl.pallas_call(
        blocks_kernel,
        out_shape=jax.ShapeDtypeStruct((4, 3, SIDE, SIDE * SIDE), F32),
        in_specs=[vmem] * 3,
        out_specs=vmem,
        compiler_params=pltpu.CompilerParams(vmem_limit_bytes=VMEM_LIMIT),
        name="to_blocks",
    )(*[p.reshape(SIDE * SIDE, LANES) for p in planes])


def solution(mesh):
    n_dev = mesh.shape["dev"]

    def local(velocity_old, viscosity_old, source):
        return to_blocks(whole(n_dev, source, velocity_old, viscosity_old))

    return jax.shard_map(
        local,
        mesh=mesh,
        in_specs=(P(("grp", "dev"), None, None, None), P(("grp", "dev"), None, None), P()),
        out_specs=P(("grp", "dev"), None, None, None),
        check_vma=False,
    )
```

```python
import functools

import jax
import jax.numpy as jnp
from jax import lax
from jax.experimental import pallas as pl
from jax.experimental.pallas import tpu as pltpu
from jax.sharding import PartitionSpec as P

F32 = jnp.float32
SIDE = 32
LANES = 128
DIFFUSION_NUMBER = 1000.0
RELAX = 0.8
BOTTOM = 8
LANE_SLOTS = (0, 2, 1, 3)
ANY = 64
H0, H1 = 4, 5
N0, N1, N2, N3 = 32, 16, 8, 4
REACH = 3
H2, H3 = REACH * N2, REACH * N3
VMEM_LIMIT = 48 * 1024 * 1024
MESH = pl.DeviceIdType.MESH
HIGHEST = lax.Precision.HIGHEST


def positions():
    grp, dev = lax.axis_index("grp"), lax.axis_index("dev")
    n_grp, n_dev = lax.axis_size("grp"), lax.axis_size("dev")
    return grp, dev, n_grp, n_dev


def stream_device(offset):
    grp, dev, n_grp, n_dev = positions()
    at = lax.rem(grp * n_dev + dev + offset + n_grp * n_dev, n_grp * n_dev)
    return (at // n_dev, lax.rem(at, n_dev))


STRIDE_TILES = 8
TOP = 8
TALL = SIDE + 2 * TOP
BODY = slice(TOP, TOP + SIDE)


def multiple(value, of):
    return pl.multiple_of(value, of)


def put(ref, n, v):
    ref[n, BODY] = v
    ref[n, :TOP] = pltpu.roll(v[SIDE - TOP :], LANES // 2, 1)
    ref[n, TOP + SIDE :] = pltpu.roll(v[:TOP], LANES // 2, 1)


def fine_beside(ref, n, v):
    return (
        pltpu.roll(v, 1, 1),
        pltpu.roll(v, LANES - 1, 1),
        ref[n, TOP - 1 : TOP + SIDE - 1],
        ref[n, TOP + 1 : TOP + SIDE + 1],
    )


def steps(lo, hi, most, body):
    count = hi - lo
    size = -(-count // -(-count // most))
    full, rest = divmod(count, size)

    def step(i, carry):
        body([lo + size * i + t for t in range(size)])
        return carry

    if full == 1:
        body(list(range(lo, lo + size)))
    else:
        lax.fori_loop(0, full, step, 0)
    if rest:
        body(list(range(hi - rest, hi)))


class Level:
    def __init__(self, rows, wide, high, d):
        self.wide, self.d = wide, d
        row = lax.broadcasted_iota(jnp.int32, (rows, LANES), 0)
        lane = lax.broadcasted_iota(jnp.int32, (rows, LANES), 1)
        deep = lax.rem(lane, high)
        self.ok_zm = deep >= d
        self.ok_zp = deep < high - d
        self.ok_ym = (row >= d) | (lane >= wide)
        self.ok_yp = (row < rows - d) | (lane < LANES - wide)
        self.wrap_m = row < d
        self.wrap_p = row >= rows - d

    def beside(self, ref, n, a):
        wide, d = self.wide, self.d
        zm = pltpu.roll(a, d, 1)
        zp = pltpu.roll(a, LANES - d, 1)
        ym = pltpu.roll(a, d, 0)
        ym = jnp.where(self.wrap_m, pltpu.roll(ym, wide, 1), ym)
        yp = pltpu.roll(a, 8 - d, 0)
        yp = jnp.where(self.wrap_p, pltpu.roll(yp, LANES - wide, 1), yp)
        return zm, zp, ym, yp


class Fine(Level):
    def beside(self, ref, n, a):
        return fine_beside(ref, n, a)


def spread_rows(a, d):
    row = lax.broadcasted_iota(jnp.int32, a.shape, 0)
    first = lax.rem(row // d, 2) == 0
    return a + jnp.where(first, pltpu.roll(a, a.shape[0] - d, 0), pltpu.roll(a, d, 0))


def spread_lanes(a, d):
    lane = lax.broadcasted_iota(jnp.int32, a.shape, 1)
    first = lax.rem(lane // d, 2) == 0
    return a + jnp.where(first, pltpu.roll(a, LANES - d, 1), pltpu.roll(a, d, 1))


def pair_sum(a, d):
    return spread_lanes(spread_rows(a, d), d)


def weights(level, coef, lo, hi, most, nu_ref, at, inside, g_ref, w_ref, iw_ref):
    def planes(ns):
        made = []
        for n in ns:
            nu = nu_ref[n, at]
            xm, xp = nu_ref[n - 1, at], nu_ref[n + 1, at]
            zm, zp, ym, yp = level.beside(nu_ref, n, nu)
            zm = jnp.where(level.ok_zm, zm, 0.0)
            zp = jnp.where(level.ok_zp, zp, 0.0)
            ym = jnp.where(level.ok_ym, ym, 0.0)
            yp = jnp.where(level.ok_yp, yp, 0.0)
            total = 6.0 * nu + ((xm + xp) + (zm + zp) + (ym + yp))
            diag = 1.0 + (0.5 * coef) * total
            w = RELAX / diag
            k = w * jnp.where(inside(n), 0.5 * coef, 0.0)
            made.append(
                (
                    n, w, diag * (1.0 / RELAX), k * (nu + xm), k * (nu + xp),
                    jnp.where(level.ok_zm, k * (nu + zm), 0.0),
                    jnp.where(level.ok_zp, k * (nu + zp), 0.0),
                    jnp.where(level.ok_ym, k * (nu + ym), 0.0),
                    jnp.where(level.ok_yp, k * (nu + yp), 0.0),
                )
            )
        for n, w, iw, *g in made:
            w_ref[n] = w
            iw_ref[n] = iw
            for i in range(6):
                g_ref[i, n] = g[i]

    steps(lo, hi, most, planes)


def gathered(level, g, src, at, n, v):
    zm, zp, ym, yp = level.beside(src, n, v)
    return (
        (g[0] * src[n - 1, at] + g[1] * src[n + 1, at])
        + (g[2] * zm + g[3] * zp)
        + (g[4] * ym + g[5] * yp)
    )


ALL = slice(None)


def sweep(level, lo, hi, most, g_ref, s_refs, srcs, store, at=ALL):
    def planes(ns):
        made = []
        for n in ns:
            g = [g_ref[i, n] for i in range(6)]
            for c, (s, src) in enumerate(zip(s_refs, srcs)):
                v = src[n, at]
                made.append(
                    (c, n, (1.0 - RELAX) * v + (s[n] + gathered(level, g, src, at, n, v)))
                )
        for c, n, v in made:
            store(c, n, v)

    steps(lo, hi, most, planes)


def storing(refs):
    def store(c, n, v):
        refs[c][n] = v

    return store


def residual(level, n, g_ref, iw_ref, s_refs, srcs, at=ALL):
    g = [g_ref[i, n] for i in range(6)]
    made = []
    for s, src in zip(s_refs, srcs):
        v = src[n, at]
        made.append(iw_ref[n] * ((s[n] + gathered(level, g, src, at, n, v)) - RELAX * v))
    return made


def names_of_scratch(n_dev):
    n0, n1, n2, n3 = N0 + 2 * H0, N1 + 2 * H1, N2 + 2 * H2, N3 + 2 * H3

    def vmem(*shape):
        return pltpu.VMEM((*shape, LANES), F32)

    def dma(*shape):
        return pltpu.SemaphoreType.DMA(shape)

    named = {"vis": pltpu.VMEM((4, SIDE, SIDE * SIDE), F32)}
    for c in range(3):
        named[f"vel{c}"] = pltpu.VMEM((4, SIDE, SIDE * SIDE), F32)
    for f in range(4):
        named[f"stage{f}"] = vmem(SIDE * SIDE)
        named[f"mid{f}"] = vmem(n_dev, STRIDE_TILES, 8)
        named[f"asm{f}"] = vmem(n_dev + 2, STRIDE_TILES + 2, 8)
        named[f"grid{f}"] = vmem(n0, TALL)
    named |= {"g0": vmem(6, n0, SIDE), "w0": vmem(n0, SIDE), "iw0": vmem(n0, SIDE)}
    for c in range(3):
        named[f"s0{c}"] = vmem(n0, SIDE)
        named[f"a0{c}"] = vmem(n0, TALL)
        named[f"b0{c}"] = vmem(n0, TALL)
    named |= {"tmp": vmem(9, SIDE), "half": vmem(4, 2, N1 + 2, 8)}
    for level, n in ((1, n1), (2, n2), (3, n3)):
        named |= {
            f"nu{level}": vmem(n, 8), f"g{level}": vmem(6, n, 8),
            f"w{level}": vmem(n, 8), f"iw{level}": vmem(n, 8),
        }
        for c in range(3):
            for kind in "xsab":
                named[f"{kind}{level}{c}"] = vmem(n, 8)
    for f in range(4):
        named[f"pack{f}"] = vmem(2 * REACH + 1, 2, 8)
    named |= {
        "in_sem": dma(4),
        "send_1": dma(4), "recv_1": dma(4), "send_2": dma(4), "recv_2": dma(4),
        "send_e": dma(4, 2), "recv_e": dma(4, 2),
        "send_p": dma(4, 2 * REACH), "recv_p": dma(4, 2 * REACH),
    }
    return named


def whole_kernel(names, source_ref, vel_hbm, vis_hbm, o_0, o_1, o_2, *scratch):
    r = dict(zip(names, scratch))
    grp, dev, n_grp, n_dev = positions()
    at = grp * n_dev + dev
    count = n_grp * n_dev
    phase, rg = dev // 4, lax.rem(dev, 4)
    hops = [k for k in range(-REACH, REACH + 1) if k]
    stages, mids = [r[f"stage{f}"] for f in range(4)], [r[f"mid{f}"] for f in range(4)]
    asms, grids = [r[f"asm{f}"] for f in range(4)], [r[f"grid{f}"] for f in range(4)]
    inputs = [r["vis"]] + [r[f"vel{c}"] for c in range(3)]

    loads = [pltpu.make_async_copy(vis_hbm, inputs[0], r["in_sem"].at[0])]
    loads += [
        pltpu.make_async_copy(vel_hbm.at[:, c], inputs[1 + c], r["in_sem"].at[1 + c])
        for c in range(3)
    ]
    for load in loads:
        load.start()
    barrier = pltpu.get_barrier_semaphore()

    def greet(t, carry):
        pl.semaphore_signal(
            barrier, inc=1, device_id=(grp, lax.rem(dev + t, n_dev)), device_id_type=MESH
        )
        return carry

    lax.fori_loop(1, n_dev, greet, 0)
    next_first = (lax.rem(grp + 1, n_grp), 0)
    before_last = (lax.rem(grp + n_grp - 1, n_grp), n_dev - 1)
    for beside in (next_first, before_last):
        pl.semaphore_signal(barrier, inc=1, device_id=beside, device_id_type=MESH)

    @pl.when(dev == 0)
    def _():
        def back(t, carry):
            pl.semaphore_signal(
                barrier, inc=1, device_id=(before_last[0], t), device_id_type=MESH
            )
            return carry

        lax.fori_loop(0, n_dev, back, 0)

    @pl.when(dev == n_dev - 1)
    def _():
        def onward(t, carry):
            pl.semaphore_signal(barrier, inc=1, device_id=(next_first[0], t), device_id_type=MESH)
            return carry

        lax.fori_loop(0, n_dev, onward, 0)

    for k in hops:
        pl.semaphore_signal(barrier, inc=1, device_id=stream_device(k), device_id_type=MESH)

    def transpose_field(f):
        for t in range(8):
            lanes = pl.ds(t * LANES, LANES)
            turned = jnp.concatenate([inputs[f][b, :, lanes] for b in LANE_SLOTS], axis=0).T
            for jj in range(4):
                stages[f][pl.ds(4 * t + jj, SIDE, stride=SIDE), :] = turned[
                    SIDE * jj : SIDE * jj + SIDE
                ]

    def spread(f):
        tiles = stages[f].reshape(STRIDE_TILES, 4, 4, 8, LANES)

        def send(t, carry):
            to = lax.rem(phase + t // 4, 4) * 4 + lax.rem(rg + lax.rem(t, 4), 4)
            pltpu.make_async_remote_copy(
                src_ref=tiles.at[:, to // 4, lax.rem(to, 4)],
                dst_ref=mids[f].at[dev],
                send_sem=r["send_1"].at[f],
                recv_sem=r["recv_1"].at[f],
                device_id=(grp, to),
                device_id_type=MESH,
            ).start()
            return carry

        pltpu.make_async_copy(tiles.at[:, phase, rg], mids[f].at[dev], r["recv_1"].at[f]).start()
        lax.fori_loop(1, n_dev, send, 0)

    group_of_lane = lax.broadcasted_iota(jnp.int32, (STRIDE_TILES, 8, LANES), 2) // SIDE
    far = STRIDE_TILES + 1

    def collect(f):
        pltpu.make_async_copy(mids[f], mids[f], r["recv_1"].at[f]).wait()
        grid = grids[f].reshape(STRIDE_TILES + 2, 4, TALL, LANES)
        asm = asms[f]

        def assemble(d, carry):
            base = (grp * n_dev + d) * 4
            made = None
            for place, slot in enumerate(LANE_SLOTS):
                old = lax.rem(source_ref[base + slot] // 4, n_dev)
                piece = mids[f][old]
                made = piece if made is None else jnp.where(group_of_lane == place, piece, made)
            asm[d + 1, 1:far] = made
            asm[d + 2, 0] = made[STRIDE_TILES - 1]
            asm[d, far] = made[0]
            return carry

        for d in range(n_dev):
            assemble(d, 0)

        def parts(d, lo, hi):
            places = pl.ds(lo, hi - lo)
            return (
                asm.at[d + 1, places],
                grid.at[places, phase, pl.ds(multiple(TOP + 8 * rg, 8), 8)],
            )

        def remote(d, lo, hi, target):
            src, dst = parts(d, lo, hi)
            pltpu.make_async_remote_copy(
                src_ref=src, dst_ref=dst, send_sem=r["send_2"].at[f], recv_sem=r["recv_2"].at[f],
                device_id=target, device_id_type=MESH,
            ).start()

        def local(d, lo, hi, target):
            src, dst = parts(d, lo, hi)
            pltpu.make_async_copy(src, dst, r["recv_2"].at[f]).start()

        def to_device(copy, d):
            @pl.when(d == 0)
            def _():
                copy(d, 1, far + 1, (grp, d))

            @pl.when(d == n_dev - 1)
            def _():
                copy(d, 0, far, (grp, d))

            @pl.when((d > 0) & (d < n_dev - 1))
            def _():
                copy(d, 0, far + 1, (grp, d))

        def send(t, carry):
            to_device(remote, lax.rem(phase + t // 4, 4) * 4 + lax.rem(rg + lax.rem(t, 4), 4))
            return carry

        lax.fori_loop(1, n_dev, send, 0)
        to_device(local, dev)
        remote(n_dev, 0, 1, next_first)
        remote(-1, far, far + 1, before_last)

    def exchange(k, src, dst, send, recv):
        return pltpu.make_async_remote_copy(
            src_ref=src, dst_ref=dst, send_sem=send, recv_sem=recv,
            device_id=stream_device(k), device_id_type=MESH,
        )

    def start(copies):
        for copy in copies:
            copy.start()
        return copies

    def wait(copies):
        for copy in copies:
            copy.wait()

    def halos(x, own, halo, send, recv, *more):
        def part(lo):
            return x.at[(pl.ds(lo, halo), *more)]

        return [
            exchange(-1, part(halo), part(halo + own), send.at[0], recv.at[0]),
            exchange(1, part(own), part(0), send.at[1], recv.at[1]),
        ]

    def grid_ready(f):
        body = grids[f].at[:, pl.ds(TOP, SIDE)]
        pltpu.make_async_copy(body, body, r["recv_2"].at[f]).wait()
        for edge, lo in ((0, 0), (count - 1, H0 + N0)):
            @pl.when(at == edge)
            def _():
                grids[f][pl.ds(lo, H0)] = jnp.zeros((H0, TALL, LANES), F32)

        def ghosts(ns):
            made = [(n, grids[f][n, BODY]) for n in ns]
            for n, v in made:
                grids[f][n, :TOP] = pltpu.roll(v[SIDE - TOP :], LANES // 2, 1)
                grids[f][n, TOP + SIDE :] = pltpu.roll(v[:TOP], LANES // 2, 1)

        steps(0, N0 + 2 * H0, 20, ghosts)

    def inside_of(own, halo):
        def inside(n):
            cell = at * own + n - halo
            return (cell >= 0) & (cell < count * own)

        return inside

    in0, in1 = inside_of(N0, H0), inside_of(N1, H1)
    in2, in3 = inside_of(N2, H2), inside_of(N3, H3)
    fine = Fine(SIDE, 2 * SIDE, 2 * SIDE, 1)
    lev1, lev2, lev3 = (Level(8, SIDE, SIDE, d) for d in (1, 2, 4))
    lane_f = lax.broadcasted_iota(jnp.int32, (LANES, LANES), 0)
    lane_c = lax.broadcasted_iota(jnp.int32, (LANES, LANES), 1)
    target = (lane_f // 64) * 64 + lax.rem(lane_f, 64) // 2
    down_m = [jnp.where(lane_c == target + 32 * jh, 0.5, 0.0).astype(F32) for jh in (0, 1)]
    target_t = (lane_c // 64) * 64 + lax.rem(lane_c, 64) // 2
    up_m = [jnp.where(lane_f == target_t + 32 * jh, 1.0, 0.0).astype(F32) for jh in (0, 1)]
    row8 = lax.broadcasted_iota(jnp.int32, (8, LANES), 0)
    lane8 = lax.broadcasted_iota(jnp.int32, (8, LANES), 1)
    tmp, half = r["tmp"], r["half"]

    def rows_halved(f, ms, totals):
        for i, total in enumerate(totals):
            tmp[i] = total
        made = [
            0.25 * (tmp[i, pl.ds(0, 16, stride=2), :] + tmp[i, pl.ds(1, 16, stride=2), :])
            for i in range(len(totals))
        ]
        for m, pairs in zip(ms, made):
            half[f, 0, m] = pairs[:8]
            half[f, 1, m] = pairs[8:]

    def lanes_halved(f):
        made = None
        for jh in (0, 1):
            part = jnp.dot(
                half[f, jh, :N1].reshape(N1 * 8, LANES), down_m[jh],
                precision=HIGHEST, preferred_element_type=F32,
            )
            made = part if made is None else made + part
        return made.reshape(N1, 8, LANES)

    def nu_pairs(ms):
        rows_halved(
            3, ms, [grids[0][H0 + 2 * m, BODY] + grids[0][H0 + 2 * m + 1, BODY] for m in ms]
        )

    def down_0(c):
        grid, s, a, b = grids[1 + c], r[f"s0{c}"], r[f"a0{c}"], r[f"b0{c}"]

        def first(ns):
            made = []
            for n in ns:
                g = [r["g0"][i, n] for i in range(6)]
                v = grid[n, BODY]
                scaled = r["w0"][n] * v
                made.append(
                    (n, scaled,
                     (1.0 - RELAX) * v + (scaled + gathered(fine, g, grid, BODY, n, v)))
                )
            for n, scaled, v in made:
                s[n] = scaled
                put(a, n, v)

        steps(1, N0 + 2 * H0 - 1, 19, first)
        sweep(
            fine, 2, N0 + 2 * H0 - 2, 18, r["g0"], [s], [a], lambda _, n, v: put(b, n, v), BODY
        )

        def pairs(ms):
            totals = []
            for m in ms:
                n = H0 + 2 * m
                [one] = residual(fine, n, r["g0"], r["iw0"], [s], [b], BODY)
                [two] = residual(fine, n + 1, r["g0"], r["iw0"], [s], [b], BODY)
                totals.append(one + two)
            rows_halved(c, ms, totals)

        steps(0, N1, 8, pairs)
        r[f"x1{c}"][pl.ds(H1, N1)] = lanes_halved(c)

    def blank(x, inside, ranges):
        for lo, hi in ranges:
            def planes(ns):
                made = [(n, jnp.where(inside(n), x[n], 0.0)) for n in ns]
                for n, v in made:
                    x[n] = v

            steps(lo, hi, 12, planes)

    def scaled(x, w, out, lo, hi):
        def planes(ns):
            made = [(n, w[n] * x[n]) for n in ns]
            for n, v in made:
                out[n] = v

        steps(lo, hi, ANY, planes)

    place = lax.rem(row8, 2) * 2 + lax.rem(lane8, 2)

    def pack(f, x):
        for h in range(N2 // 4):
            made = x[H2 + 4 * h]
            for p in range(1, 4):
                made = jnp.where(place == p, x[H2 + 4 * h + p], made)
            r[f"pack{f}"][REACH, h] = made
        packed = r[f"pack{f}"]
        return start(
            [
                exchange(
                    k, packed.at[REACH], packed.at[REACH - k],
                    r["send_p"].at[f, i], r["recv_p"].at[f, i],
                )
                for i, k in enumerate(hops)
            ]
        )

    def unpack(f, x, moving):
        wait(moving)

        def blocks(bs):
            made = []
            for b in bs:
                for h in range(N2 // 4):
                    packed = r[f"pack{f}"][b, h]
                    for p in range(4):
                        n = N2 * b + 4 * h + p
                        one = jnp.where((place == p) & in2(n), packed, 0.0)
                        made.append((n, pair_sum(one, 1)))
            for n, v in made:
                x[n] = v

        steps(0, REACH, ANY, blocks)
        steps(REACH + 1, 2 * REACH + 1, ANY, blocks)

    nu1, nu2, nu3 = r["nu1"], r["nu2"], r["nu3"]

    def nu_down(fine_nu, coarse_nu, halo_f, halo_c, d):
        def planes(ms):
            made = [
                (m, 0.125 * pair_sum(fine_nu[halo_f + 2 * m] + fine_nu[halo_f + 2 * m + 1], d))
                for m in ms
            ]
            for m, v in made:
                coarse_nu[halo_c + m] = v

        return planes

    def to_level_1(c):
        send, recv = r["send_e"].at[1 + c], r["recv_e"].at[1 + c]
        return start(halos(r[f"x1{c}"], N1, H1, send, recv))

    def staged(f):
        loads[f].wait()
        transpose_field(f)

    for f in range(4):
        staged(f)
    ends = jnp.where((dev == 0) | (dev == n_dev - 1), n_dev, 0)
    pl.semaphore_wait(barrier, n_dev - 1 + len(hops) + 2 + ends)
    spread(0)
    spread(1)
    collect(0)
    spread(2)
    collect(1)
    spread(3)
    collect(2)

    grid_ready(0)
    steps(0, N1, 8, nu_pairs)
    nu1[pl.ds(H1, N1)] = lanes_halved(3)
    moving = start(halos(nu1, N1, H1, r["send_e"].at[0], r["recv_e"].at[0]))
    collect(3)
    weights(
        fine, DIFFUSION_NUMBER, 1, N0 + 2 * H0 - 1, 10, grids[0], BODY, in0, r["g0"], r["w0"],
        r["iw0"],
    )
    wait(moving)
    blank(nu1, in1, [(0, H1), (H1 + N1, N1 + 2 * H1)])
    steps(0, N2, 8, nu_down(nu1, nu2, H1, H2, 1))
    moving = pack(3, nu2)
    weights(
        lev1, DIFFUSION_NUMBER / 4, 1, N1 + 2 * H1 - 1, ANY, nu1, ALL, in1, r["g1"], r["w1"], r["iw1"]
    )
    grid_ready(1)
    down_0(0)
    first = to_level_1(0)
    lo3 = H3 - 2 - (BOTTOM - 1)
    hi3 = N3 + 2 * H3 - lo3
    lo2, hi2 = 2 * lo3 - 2, 2 * hi3 + 2

    def down(level, ms, start_f, start_c, g, iw, s, a, x, d):
        made = []
        for m in ms:
            n = start_f + 2 * m
            [one] = residual(level, n, g, iw, [s], [a])
            [two] = residual(level, n + 1, g, iw, [s], [a])
            made.append((m, 0.125 * pair_sum(one + two, d)))
        for m, v in made:
            x[start_c + m] = v

    def to_level_2(c, moving):
        x, s, a = r[f"x1{c}"], r[f"s1{c}"], r[f"a1{c}"]
        wait(moving)
        blank(x, in1, [(0, H1), (H1 + N1, N1 + 2 * H1)])
        scaled(x, r["w1"], s, 1, N1 + 2 * H1 - 1)
        sweep(lev1, 2, N1 + 2 * H1 - 2, ANY, r["g1"], [s], [s], storing([a]))
        steps(
            0, N2, ANY,
            lambda ms: down(lev1, ms, H1, H2, r["g1"], r["iw1"], s, a, r[f"x2{c}"], 1),
        )
        return pack(c, r[f"x2{c}"])

    def add(b, coarse, start_f, start_c):
        def pairs(ms):
            made = []
            for m in ms:
                more = coarse[start_c + m]
                for twin in (0, 1):
                    n = start_f + 2 * m + twin
                    made.append((n, b[n] + more))
            for n, v in made:
                b[n] = v

        return pairs

    def bottom(c, moving):
        x, s, a, b = (r[f"{kind}2{c}"] for kind in "xsab")
        unpack(c, x, moving)
        scaled(x, r["w2"], s, lo2, hi2)
        sweep(lev2, lo2 + 1, hi2 - 1, ANY, r["g2"], [s], [s], storing([a]))
        x3, s3, a3, b3 = (r[f"{kind}3{c}"] for kind in "xsab")
        steps(
            lo3, hi3, ANY, lambda ms: down(lev2, ms, 0, 0, r["g2"], r["iw2"], s, a, x3, 2)
        )
        scaled(x3, r["w3"], s3, lo3, hi3)
        src = s3
        for turn in range(1, BOTTOM):
            dst = a3 if turn % 2 else b3
            sweep(lev3, lo3 + turn, hi3 - turn, ANY, r["g3"], [s3], [src], storing([dst]))
            src = dst
        steps(0, (N2 + 8) // 2, ANY, add(a, src, H2 - 4, H3 - 2))
        sweep(lev2, H2 - 3, H2 + N2 + 3, ANY, r["g2"], [s], [a], storing([b]))
        sweep(lev2, H2 - 2, H2 + N2 + 2, ANY, r["g2"], [s], [b], storing([a]))
        s1, a1, b1 = (r[f"{kind}1{c}"] for kind in "sab")
        steps(0, (N1 + 8) // 2, ANY, add(a1, a, H1 - 4, H2 - 2))
        sweep(lev1, 3, N1 + 2 * H1 - 3, ANY, r["g1"], [s1], [a1], storing([b1]))
        sweep(lev1, 4, N1 + 2 * H1 - 4, ANY, r["g1"], [s1], [b1], storing([a1]))

    outs = (o_0, o_1, o_2)

    def top(c):
        wide = N1 + 2
        coarse = r[f"a1{c}"][pl.ds(H1 - 1, wide)].reshape(wide * 8, LANES)
        for jh in (0, 1):
            half[c, jh] = jnp.dot(
                coarse, up_m[jh], precision=HIGHEST, preferred_element_type=F32
            ).reshape(wide, 8, LANES)
        s, a, b = r[f"s0{c}"], r[f"a0{c}"], r[f"b0{c}"]

        def refined(ms):
            for i, m in enumerate(ms):
                for jh in (0, 1):
                    for twin in (0, 1):
                        tmp[i, pl.ds(16 * jh + twin, 8, stride=2), :] = half[c, jh, m]
            made = []
            for i, m in enumerate(ms):
                for twin in (0, 1):
                    n = H0 - 2 + 2 * m + twin
                    made.append((n, b[n, BODY] + tmp[i]))
            for n, v in made:
                put(b, n, v)

        steps(0, wide, 9, refined)
        sweep(
            fine, 3, N0 + 2 * H0 - 3, 17, r["g0"], [s], [b], lambda _, n, v: put(a, n, v), BODY
        )

        def to_out(_, n, v):
            outs[c][n - H0] = v

        sweep(fine, 4, N0 + 2 * H0 - 4, 16, r["g0"], [s], [a], to_out, BODY)

    first = to_level_2(0, first)
    grid_ready(2)
    down_0(1)
    second = to_level_1(1)
    unpack(3, nu2, moving)
    steps(lo3 - 1, hi3 + 1, 12, nu_down(nu2, nu3, 0, 0, 2))
    weights(
        lev2, DIFFUSION_NUMBER / 16, lo2, hi2, 24, nu2, ALL, in2, r["g2"], r["w2"], r["iw2"]
    )
    weights(
        lev3, DIFFUSION_NUMBER / 64, lo3, hi3, ANY, nu3, ALL, in3, r["g3"], r["w3"], r["iw3"]
    )
    second = to_level_2(1, second)
    grid_ready(3)
    down_0(2)
    third = to_level_1(2)
    bottom(0, first)
    bottom(1, second)
    third = to_level_2(2, third)
    top(0)
    top(1)
    bottom(2, third)
    top(2)

    for f in range(4):
        most = mids[f].at[pl.ds(0, n_dev - 1)]
        pltpu.make_async_copy(most, most, r["send_1"].at[f]).wait()

        @pl.when((dev > 0) & (dev < n_dev - 1))
        def _():
            most = asms[f].at[pl.ds(0, n_dev - 1)]
            pltpu.make_async_copy(most, most, r["send_2"].at[f]).wait()

        @pl.when((dev == 0) | (dev == n_dev - 1))
        def _():
            most = stages[f].reshape(SIDE * SIDE // 8, 8, LANES).at[pl.ds(0, 128)]
            pltpu.make_async_copy(most, most, r["send_2"].at[f]).wait()
            rest = stages[f].reshape(SIDE * SIDE // 8, 8, LANES).at[pl.ds(0, 23)]
            pltpu.make_async_copy(rest, rest, r["send_2"].at[f]).wait()


def whole(n_dev, source, velocity_old, viscosity_old):
    vmem = pl.BlockSpec(memory_space=pltpu.VMEM)
    anywhere = pl.BlockSpec(memory_space=pltpu.HBM)
    named = names_of_scratch(n_dev)
    return pl.pallas_call(
        functools.partial(whole_kernel, tuple(named)),
        out_shape=[jax.ShapeDtypeStruct((N0, SIDE, LANES), F32)] * 3,
        in_specs=[pl.BlockSpec(memory_space=pltpu.SMEM), anywhere, anywhere],
        out_specs=[vmem] * 3,
        scratch_shapes=list(named.values()),
        compiler_params=pltpu.CompilerParams(
            collective_id=0, has_side_effects=True, vmem_limit_bytes=VMEM_LIMIT
        ),
        name="whole",
    )(source, velocity_old, viscosity_old)


def blocks_kernel(e_0, e_1, e_2, out_ref):
    for c, e in enumerate((e_0, e_1, e_2)):
        for t in range(8):
            parts = [e[pl.ds(4 * t + jj, SIDE, stride=SIDE), :] for jj in range(4)]
            turned = jnp.concatenate(parts, axis=0).T
            for at, slot in enumerate(LANE_SLOTS):
                out_ref[slot, c, :, pl.ds(t * LANES, LANES)] = turned[SIDE * at : SIDE * at + SIDE]


def to_blocks(planes):
    vmem = pl.BlockSpec(memory_space=pltpu.VMEM)
    return pl.pallas_call(
        blocks_kernel,
        out_shape=jax.ShapeDtypeStruct((4, 3, SIDE, SIDE * SIDE), F32),
        in_specs=[vmem] * 3,
        out_specs=vmem,
        compiler_params=pltpu.CompilerParams(vmem_limit_bytes=VMEM_LIMIT),
        name="to_blocks",
    )(*[p.reshape(SIDE * SIDE, LANES) for p in planes])


def solution(mesh):
    n_dev = mesh.shape["dev"]

    def local(velocity_old, viscosity_old, source):
        return to_blocks(whole(n_dev, source, velocity_old, viscosity_old))

    return jax.shard_map(
        local,
        mesh=mesh,
        in_specs=(P(("grp", "dev"), None, None, None), P(("grp", "dev"), None, None), P()),
        out_specs=P(("grp", "dev"), None, None, None),
        check_vma=False,
    )
```

```python
import functools

import jax
import jax.numpy as jnp
from jax import lax
from jax.experimental import pallas as pl
from jax.experimental.pallas import tpu as pltpu
from jax.sharding import PartitionSpec as P

F32 = jnp.float32
SIDE = 32
LANES = 128
DIFFUSION_NUMBER = 1000.0
RELAX = 0.8
BOTTOM = 8
LANE_SLOTS = (0, 2, 1, 3)
ANY = 64
H0, H1 = 4, 5
N0, N1, N2, N3 = 32, 16, 8, 4
REACH = 3
H2, H3 = REACH * N2, REACH * N3
VMEM_LIMIT = 48 * 1024 * 1024
MESH = pl.DeviceIdType.MESH
HIGHEST = lax.Precision.HIGHEST


def positions():
    grp, dev = lax.axis_index("grp"), lax.axis_index("dev")
    n_grp, n_dev = lax.axis_size("grp"), lax.axis_size("dev")
    return grp, dev, n_grp, n_dev


def stream_device(offset):
    grp, dev, n_grp, n_dev = positions()
    at = lax.rem(grp * n_dev + dev + offset + n_grp * n_dev, n_grp * n_dev)
    return (at // n_dev, lax.rem(at, n_dev))


STRIDE_TILES = 8
TOP = 8
TALL = SIDE + 2 * TOP
BODY = slice(TOP, TOP + SIDE)


def multiple(value, of):
    return pl.multiple_of(value, of)


def put(ref, n, v):
    ref[n, BODY] = v
    ref[n, :TOP] = pltpu.roll(v[SIDE - TOP :], LANES // 2, 1)
    ref[n, TOP + SIDE :] = pltpu.roll(v[:TOP], LANES // 2, 1)


def fine_beside(ref, n, v):
    return (
        pltpu.roll(v, 1, 1),
        pltpu.roll(v, LANES - 1, 1),
        ref[n, TOP - 1 : TOP + SIDE - 1],
        ref[n, TOP + 1 : TOP + SIDE + 1],
    )


def steps(lo, hi, most, body):
    count = hi - lo
    size = -(-count // -(-count // most))
    full, rest = divmod(count, size)

    def step(i, carry):
        body([lo + size * i + t for t in range(size)])
        return carry

    if full == 1:
        body(list(range(lo, lo + size)))
    else:
        lax.fori_loop(0, full, step, 0)
    if rest:
        body(list(range(hi - rest, hi)))


class Level:
    def __init__(self, rows, wide, high, d):
        self.wide, self.d = wide, d
        row = lax.broadcasted_iota(jnp.int32, (rows, LANES), 0)
        lane = lax.broadcasted_iota(jnp.int32, (rows, LANES), 1)
        deep = lax.rem(lane, high)
        self.ok_zm = deep >= d
        self.ok_zp = deep < high - d
        self.ok_ym = (row >= d) | (lane >= wide)
        self.ok_yp = (row < rows - d) | (lane < LANES - wide)
        self.wrap_m = row < d
        self.wrap_p = row >= rows - d

    def beside(self, ref, n, a):
        wide, d = self.wide, self.d
        zm = pltpu.roll(a, d, 1)
        zp = pltpu.roll(a, LANES - d, 1)
        ym = pltpu.roll(a, d, 0)
        ym = jnp.where(self.wrap_m, pltpu.roll(ym, wide, 1), ym)
        yp = pltpu.roll(a, 8 - d, 0)
        yp = jnp.where(self.wrap_p, pltpu.roll(yp, LANES - wide, 1), yp)
        return zm, zp, ym, yp


class Fine(Level):
    def beside(self, ref, n, a):
        return fine_beside(ref, n, a)


def spread_rows(a, d):
    row = lax.broadcasted_iota(jnp.int32, a.shape, 0)
    first = lax.rem(row // d, 2) == 0
    return a + jnp.where(first, pltpu.roll(a, a.shape[0] - d, 0), pltpu.roll(a, d, 0))


def spread_lanes(a, d):
    lane = lax.broadcasted_iota(jnp.int32, a.shape, 1)
    first = lax.rem(lane // d, 2) == 0
    return a + jnp.where(first, pltpu.roll(a, LANES - d, 1), pltpu.roll(a, d, 1))


def pair_sum(a, d):
    return spread_lanes(spread_rows(a, d), d)


def weights(level, coef, lo, hi, most, nu_ref, at, inside, g_ref, w_ref, iw_ref):
    def planes(ns):
        made = []
        for n in ns:
            nu = nu_ref[n, at]
            xm, xp = nu_ref[n - 1, at], nu_ref[n + 1, at]
            zm, zp, ym, yp = level.beside(nu_ref, n, nu)
            zm = jnp.where(level.ok_zm, zm, 0.0)
            zp = jnp.where(level.ok_zp, zp, 0.0)
            ym = jnp.where(level.ok_ym, ym, 0.0)
            yp = jnp.where(level.ok_yp, yp, 0.0)
            total = 6.0 * nu + ((xm + xp) + (zm + zp) + (ym + yp))
            diag = 1.0 + (0.5 * coef) * total
            w = RELAX / diag
            k = w * jnp.where(inside(n), 0.5 * coef, 0.0)
            made.append(
                (
                    n, w, diag * (1.0 / RELAX), k * (nu + xm), k * (nu + xp),
                    jnp.where(level.ok_zm, k * (nu + zm), 0.0),
                    jnp.where(level.ok_zp, k * (nu + zp), 0.0),
                    jnp.where(level.ok_ym, k * (nu + ym), 0.0),
                    jnp.where(level.ok_yp, k * (nu + yp), 0.0),
                )
            )
        for n, w, iw, *g in made:
            w_ref[n] = w
            iw_ref[n] = iw
            for i in range(6):
                g_ref[i, n] = g[i]

    steps(lo, hi, most, planes)


def gathered(level, g, src, at, n, v):
    zm, zp, ym, yp = level.beside(src, n, v)
    return (
        (g[0] * src[n - 1, at] + g[1] * src[n + 1, at])
        + (g[2] * zm + g[3] * zp)
        + (g[4] * ym + g[5] * yp)
    )


ALL = slice(None)


def sweep(level, lo, hi, most, g_ref, s_refs, srcs, store, at=ALL):
    def planes(ns):
        made = []
        for n in ns:
            g = [g_ref[i, n] for i in range(6)]
            for c, (s, src) in enumerate(zip(s_refs, srcs)):
                v = src[n, at]
                made.append(
                    (c, n, (1.0 - RELAX) * v + (s[n] + gathered(level, g, src, at, n, v)))
                )
        for c, n, v in made:
            store(c, n, v)

    steps(lo, hi, most, planes)


def storing(refs):
    def store(c, n, v):
        refs[c][n] = v

    return store


def residual(level, n, g_ref, iw_ref, s_refs, srcs, at=ALL):
    g = [g_ref[i, n] for i in range(6)]
    made = []
    for s, src in zip(s_refs, srcs):
        v = src[n, at]
        made.append(iw_ref[n] * ((s[n] + gathered(level, g, src, at, n, v)) - RELAX * v))
    return made


def names_of_scratch(n_dev):
    n0, n1, n2, n3 = N0 + 2 * H0, N1 + 2 * H1, N2 + 2 * H2, N3 + 2 * H3

    def vmem(*shape):
        return pltpu.VMEM((*shape, LANES), F32)

    def dma(*shape):
        return pltpu.SemaphoreType.DMA(shape)

    named = {"vis": pltpu.VMEM((4, SIDE, SIDE * SIDE), F32)}
    for c in range(3):
        named[f"vel{c}"] = pltpu.VMEM((4, SIDE, SIDE * SIDE), F32)
    for f in range(4):
        named[f"stage{f}"] = vmem(SIDE * SIDE)
        named[f"mid{f}"] = vmem(n_dev, STRIDE_TILES, 8)
        named[f"asm{f}"] = vmem(n_dev + 2, STRIDE_TILES + 2, 8)
        named[f"grid{f}"] = vmem(n0, TALL)
    named |= {"g0": vmem(6, n0, SIDE), "w0": vmem(n0, SIDE), "iw0": vmem(n0, SIDE)}
    for c in range(3):
        named[f"s0{c}"] = vmem(n0, SIDE)
        named[f"a0{c}"] = vmem(n0, TALL)
        named[f"b0{c}"] = vmem(n0, TALL)
    named |= {"tmp": vmem(9, SIDE), "half": vmem(4, 2, N1 + 2, 8)}
    for level, n in ((1, n1), (2, n2), (3, n3)):
        named |= {
            f"nu{level}": vmem(n, 8), f"g{level}": vmem(6, n, 8),
            f"w{level}": vmem(n, 8), f"iw{level}": vmem(n, 8),
        }
        for c in range(3):
            for kind in "xsab":
                named[f"{kind}{level}{c}"] = vmem(n, 8)
    for f in range(4):
        named[f"pack{f}"] = vmem(2 * REACH + 1, 2, 8)
    named |= {
        "in_sem": dma(4),
        "send_1": dma(4), "recv_1": dma(4), "send_2": dma(4), "recv_2": dma(4),
        "send_e": dma(4, 2), "recv_e": dma(4, 2),
        "send_p": dma(4, 2 * REACH), "recv_p": dma(4, 2 * REACH),
    }
    return named


def whole_kernel(names, source_ref, vel_hbm, vis_hbm, o_0, o_1, o_2, *scratch):
    r = dict(zip(names, scratch))
    grp, dev, n_grp, n_dev = positions()
    at = grp * n_dev + dev
    count = n_grp * n_dev
    phase, rg = dev // 4, lax.rem(dev, 4)
    hops = [k for k in range(-REACH, REACH + 1) if k]
    stages, mids = [r[f"stage{f}"] for f in range(4)], [r[f"mid{f}"] for f in range(4)]
    asms, grids = [r[f"asm{f}"] for f in range(4)], [r[f"grid{f}"] for f in range(4)]
    inputs = [r["vis"]] + [r[f"vel{c}"] for c in range(3)]

    loads = [pltpu.make_async_copy(vis_hbm, inputs[0], r["in_sem"].at[0])]
    loads += [
        pltpu.make_async_copy(vel_hbm.at[:, c], inputs[1 + c], r["in_sem"].at[1 + c])
        for c in range(3)
    ]
    for load in loads:
        load.start()
    barrier = pltpu.get_barrier_semaphore()

    def greet(t, carry):
        pl.semaphore_signal(
            barrier, inc=1, device_id=(grp, lax.rem(dev + t, n_dev)), device_id_type=MESH
        )
        return carry

    lax.fori_loop(1, n_dev, greet, 0)
    next_first = (lax.rem(grp + 1, n_grp), 0)
    before_last = (lax.rem(grp + n_grp - 1, n_grp), n_dev - 1)
    for beside in (next_first, before_last):
        pl.semaphore_signal(barrier, inc=1, device_id=beside, device_id_type=MESH)

    @pl.when(dev == 0)
    def _():
        def back(t, carry):
            pl.semaphore_signal(
                barrier, inc=1, device_id=(before_last[0], t), device_id_type=MESH
            )
            return carry

        lax.fori_loop(0, n_dev, back, 0)

    @pl.when(dev == n_dev - 1)
    def _():
        def onward(t, carry):
            pl.semaphore_signal(barrier, inc=1, device_id=(next_first[0], t), device_id_type=MESH)
            return carry

        lax.fori_loop(0, n_dev, onward, 0)

    crossing = 0
    for k in hops:
        outside = (dev + k < 0) | (dev + k >= n_dev)
        crossing = crossing + jnp.where(outside, 1, 0)

        @pl.when(outside)
        def _(k=k):
            pl.semaphore_signal(barrier, inc=1, device_id=stream_device(k), device_id_type=MESH)

    def transpose_field(f):
        for t in range(8):
            lanes = pl.ds(t * LANES, LANES)
            turned = jnp.concatenate([inputs[f][b, :, lanes] for b in LANE_SLOTS], axis=0).T
            for jj in range(4):
                stages[f][pl.ds(4 * t + jj, SIDE, stride=SIDE), :] = turned[
                    SIDE * jj : SIDE * jj + SIDE
                ]

    def spread(f):
        tiles = stages[f].reshape(STRIDE_TILES, 4, 4, 8, LANES)

        def send(t, carry):
            to = lax.rem(dev + t, n_dev)
            pltpu.make_async_remote_copy(
                src_ref=tiles.at[:, to // 4, lax.rem(to, 4)],
                dst_ref=mids[f].at[dev],
                send_sem=r["send_1"].at[f],
                recv_sem=r["recv_1"].at[f],
                device_id=(grp, to),
                device_id_type=MESH,
            ).start()
            return carry

        pltpu.make_async_copy(tiles.at[:, phase, rg], mids[f].at[dev], r["recv_1"].at[f]).start()
        lax.fori_loop(1, n_dev, send, 0)

    group_of_lane = lax.broadcasted_iota(jnp.int32, (STRIDE_TILES, 8, LANES), 2) // SIDE
    far = STRIDE_TILES + 1

    def collect(f):
        pltpu.make_async_copy(mids[f], mids[f], r["recv_1"].at[f]).wait()
        grid = grids[f].reshape(STRIDE_TILES + 2, 4, TALL, LANES)
        asm = asms[f]

        def assemble(d, carry):
            base = (grp * n_dev + d) * 4
            made = None
            for place, slot in enumerate(LANE_SLOTS):
                old = lax.rem(source_ref[base + slot] // 4, n_dev)
                piece = mids[f][old]
                made = piece if made is None else jnp.where(group_of_lane == place, piece, made)
            asm[d + 1, 1:far] = made
            asm[d + 2, 0] = made[STRIDE_TILES - 1]
            asm[d, far] = made[0]
            return carry

        for d in range(n_dev):
            assemble(d, 0)

        def parts(d, lo, hi):
            places = pl.ds(lo, hi - lo)
            return (
                asm.at[d + 1, places],
                grid.at[places, phase, pl.ds(multiple(TOP + 8 * rg, 8), 8)],
            )

        def remote(d, lo, hi, target):
            src, dst = parts(d, lo, hi)
            pltpu.make_async_remote_copy(
                src_ref=src, dst_ref=dst, send_sem=r["send_2"].at[f], recv_sem=r["recv_2"].at[f],
                device_id=target, device_id_type=MESH,
            ).start()

        def local(d, lo, hi, target):
            src, dst = parts(d, lo, hi)
            pltpu.make_async_copy(src, dst, r["recv_2"].at[f]).start()

        def to_device(copy, d):
            @pl.when(d == 0)
            def _():
                copy(d, 1, far + 1, (grp, d))

            @pl.when(d == n_dev - 1)
            def _():
                copy(d, 0, far, (grp, d))

            @pl.when((d > 0) & (d < n_dev - 1))
            def _():
                copy(d, 0, far + 1, (grp, d))

        def send(t, carry):
            to_device(remote, lax.rem(dev + t, n_dev))
            return carry

        lax.fori_loop(1, n_dev, send, 0)
        to_device(local, dev)
        remote(n_dev, 0, 1, next_first)
        remote(-1, far, far + 1, before_last)

    def exchange(k, src, dst, send, recv):
        return pltpu.make_async_remote_copy(
            src_ref=src, dst_ref=dst, send_sem=send, recv_sem=recv,
            device_id=stream_device(k), device_id_type=MESH,
        )

    def start(copies):
        for copy in copies:
            copy.start()
        return copies

    def wait(copies):
        for copy in copies:
            copy.wait()

    def halos(x, own, halo, send, recv, *more):
        def part(lo):
            return x.at[(pl.ds(lo, halo), *more)]

        return [
            exchange(-1, part(halo), part(halo + own), send.at[0], recv.at[0]),
            exchange(1, part(own), part(0), send.at[1], recv.at[1]),
        ]

    def grid_ready(f):
        body = grids[f].at[:, pl.ds(TOP, SIDE)]
        pltpu.make_async_copy(body, body, r["recv_2"].at[f]).wait()
        for edge, lo in ((0, 0), (count - 1, H0 + N0)):
            @pl.when(at == edge)
            def _():
                grids[f][pl.ds(lo, H0)] = jnp.zeros((H0, TALL, LANES), F32)

        def ghosts(ns):
            made = [(n, grids[f][n, BODY]) for n in ns]
            for n, v in made:
                grids[f][n, :TOP] = pltpu.roll(v[SIDE - TOP :], LANES // 2, 1)
                grids[f][n, TOP + SIDE :] = pltpu.roll(v[:TOP], LANES // 2, 1)

        steps(0, N0 + 2 * H0, 20, ghosts)

    def inside_of(own, halo):
        def inside(n):
            cell = at * own + n - halo
            return (cell >= 0) & (cell < count * own)

        return inside

    in0, in1 = inside_of(N0, H0), inside_of(N1, H1)
    in2, in3 = inside_of(N2, H2), inside_of(N3, H3)
    fine = Fine(SIDE, 2 * SIDE, 2 * SIDE, 1)
    lev1, lev2, lev3 = (Level(8, SIDE, SIDE, d) for d in (1, 2, 4))
    lane_f = lax.broadcasted_iota(jnp.int32, (LANES, LANES), 0)
    lane_c = lax.broadcasted_iota(jnp.int32, (LANES, LANES), 1)
    target = (lane_f // 64) * 64 + lax.rem(lane_f, 64) // 2
    down_m = [jnp.where(lane_c == target + 32 * jh, 0.5, 0.0).astype(F32) for jh in (0, 1)]
    target_t = (lane_c // 64) * 64 + lax.rem(lane_c, 64) // 2
    up_m = [jnp.where(lane_f == target_t + 32 * jh, 1.0, 0.0).astype(F32) for jh in (0, 1)]
    row8 = lax.broadcasted_iota(jnp.int32, (8, LANES), 0)
    lane8 = lax.broadcasted_iota(jnp.int32, (8, LANES), 1)
    tmp, half = r["tmp"], r["half"]

    def rows_halved(f, ms, totals):
        for i, total in enumerate(totals):
            tmp[i] = total
        made = [
            0.25 * (tmp[i, pl.ds(0, 16, stride=2), :] + tmp[i, pl.ds(1, 16, stride=2), :])
            for i in range(len(totals))
        ]
        for m, pairs in zip(ms, made):
            half[f, 0, m] = pairs[:8]
            half[f, 1, m] = pairs[8:]

    def lanes_halved(f):
        made = None
        for jh in (0, 1):
            part = jnp.dot(
                half[f, jh, :N1].reshape(N1 * 8, LANES), down_m[jh],
                precision=HIGHEST, preferred_element_type=F32,
            )
            made = part if made is None else made + part
        return made.reshape(N1, 8, LANES)

    def nu_pairs(ms):
        rows_halved(
            3, ms, [grids[0][H0 + 2 * m, BODY] + grids[0][H0 + 2 * m + 1, BODY] for m in ms]
        )

    def down_0(c):
        grid, s, a, b = grids[1 + c], r[f"s0{c}"], r[f"a0{c}"], r[f"b0{c}"]

        def first(ns):
            made = []
            for n in ns:
                g = [r["g0"][i, n] for i in range(6)]
                v = grid[n, BODY]
                scaled = r["w0"][n] * v
                made.append(
                    (n, scaled,
                     (1.0 - RELAX) * v + (scaled + gathered(fine, g, grid, BODY, n, v)))
                )
            for n, scaled, v in made:
                s[n] = scaled
                put(a, n, v)

        steps(1, N0 + 2 * H0 - 1, 19, first)
        sweep(
            fine, 2, N0 + 2 * H0 - 2, 18, r["g0"], [s], [a], lambda _, n, v: put(b, n, v), BODY
        )

        def pairs(ms):
            totals = []
            for m in ms:
                n = H0 + 2 * m
                [one] = residual(fine, n, r["g0"], r["iw0"], [s], [b], BODY)
                [two] = residual(fine, n + 1, r["g0"], r["iw0"], [s], [b], BODY)
                totals.append(one + two)
            rows_halved(c, ms, totals)

        steps(0, N1, 8, pairs)
        r[f"x1{c}"][pl.ds(H1, N1)] = lanes_halved(c)

    def blank(x, inside, ranges):
        for lo, hi in ranges:
            def planes(ns):
                made = [(n, jnp.where(inside(n), x[n], 0.0)) for n in ns]
                for n, v in made:
                    x[n] = v

            steps(lo, hi, 12, planes)

    def scaled(x, w, out, lo, hi):
        def planes(ns):
            made = [(n, w[n] * x[n]) for n in ns]
            for n, v in made:
                out[n] = v

        steps(lo, hi, ANY, planes)

    place = lax.rem(row8, 2) * 2 + lax.rem(lane8, 2)

    def pack(f, x):
        for h in range(N2 // 4):
            made = x[H2 + 4 * h]
            for p in range(1, 4):
                made = jnp.where(place == p, x[H2 + 4 * h + p], made)
            r[f"pack{f}"][REACH, h] = made
        packed = r[f"pack{f}"]
        return start(
            [
                exchange(
                    k, packed.at[REACH], packed.at[REACH - k],
                    r["send_p"].at[f, i], r["recv_p"].at[f, i],
                )
                for i, k in enumerate(hops)
            ]
        )

    def unpack(f, x, moving):
        wait(moving)

        def blocks(bs):
            made = []
            for b in bs:
                for h in range(N2 // 4):
                    packed = r[f"pack{f}"][b, h]
                    for p in range(4):
                        n = N2 * b + 4 * h + p
                        one = jnp.where((place == p) & in2(n), packed, 0.0)
                        made.append((n, pair_sum(one, 1)))
            for n, v in made:
                x[n] = v

        steps(0, REACH, ANY, blocks)
        steps(REACH + 1, 2 * REACH + 1, ANY, blocks)

    nu1, nu2, nu3 = r["nu1"], r["nu2"], r["nu3"]

    def nu_down(fine_nu, coarse_nu, halo_f, halo_c, d):
        def planes(ms):
            made = [
                (m, 0.125 * pair_sum(fine_nu[halo_f + 2 * m] + fine_nu[halo_f + 2 * m + 1], d))
                for m in ms
            ]
            for m, v in made:
                coarse_nu[halo_c + m] = v

        return planes

    def to_level_1(c):
        send, recv = r["send_e"].at[1 + c], r["recv_e"].at[1 + c]
        return start(halos(r[f"x1{c}"], N1, H1, send, recv))

    def staged(f):
        loads[f].wait()
        transpose_field(f)

    for f in range(4):
        staged(f)
    ends = jnp.where((dev == 0) | (dev == n_dev - 1), n_dev, 0)
    pl.semaphore_wait(barrier, n_dev - 1 + crossing + 2 + ends)
    spread(0)
    spread(1)
    collect(0)
    spread(2)
    collect(1)
    spread(3)
    collect(2)

    grid_ready(0)
    steps(0, N1, 8, nu_pairs)
    nu1[pl.ds(H1, N1)] = lanes_halved(3)
    moving = start(halos(nu1, N1, H1, r["send_e"].at[0], r["recv_e"].at[0]))
    collect(3)
    weights(
        fine, DIFFUSION_NUMBER, 1, N0 + 2 * H0 - 1, 10, grids[0], BODY, in0, r["g0"], r["w0"],
        r["iw0"],
    )
    wait(moving)
    blank(nu1, in1, [(0, H1), (H1 + N1, N1 + 2 * H1)])
    steps(0, N2, 8, nu_down(nu1, nu2, H1, H2, 1))
    moving = pack(3, nu2)
    weights(
        lev1, DIFFUSION_NUMBER / 4, 1, N1 + 2 * H1 - 1, ANY, nu1, ALL, in1, r["g1"], r["w1"], r["iw1"]
    )
    grid_ready(1)
    down_0(0)
    first = to_level_1(0)
    lo3 = H3 - 2 - (BOTTOM - 1)
    hi3 = N3 + 2 * H3 - lo3
    lo2, hi2 = 2 * lo3 - 2, 2 * hi3 + 2

    def down(level, ms, start_f, start_c, g, iw, s, a, x, d):
        made = []
        for m in ms:
            n = start_f + 2 * m
            [one] = residual(level, n, g, iw, [s], [a])
            [two] = residual(level, n + 1, g, iw, [s], [a])
            made.append((m, 0.125 * pair_sum(one + two, d)))
        for m, v in made:
            x[start_c + m] = v

    def to_level_2(c, moving):
        x, s, a = r[f"x1{c}"], r[f"s1{c}"], r[f"a1{c}"]
        wait(moving)
        blank(x, in1, [(0, H1), (H1 + N1, N1 + 2 * H1)])
        scaled(x, r["w1"], s, 1, N1 + 2 * H1 - 1)
        sweep(lev1, 2, N1 + 2 * H1 - 2, ANY, r["g1"], [s], [s], storing([a]))
        steps(
            0, N2, ANY,
            lambda ms: down(lev1, ms, H1, H2, r["g1"], r["iw1"], s, a, r[f"x2{c}"], 1),
        )
        return pack(c, r[f"x2{c}"])

    def add(b, coarse, start_f, start_c):
        def pairs(ms):
            made = []
            for m in ms:
                more = coarse[start_c + m]
                for twin in (0, 1):
                    n = start_f + 2 * m + twin
                    made.append((n, b[n] + more))
            for n, v in made:
                b[n] = v

        return pairs

    def bottom(c, moving):
        x, s, a, b = (r[f"{kind}2{c}"] for kind in "xsab")
        unpack(c, x, moving)
        scaled(x, r["w2"], s, lo2, hi2)
        sweep(lev2, lo2 + 1, hi2 - 1, ANY, r["g2"], [s], [s], storing([a]))
        x3, s3, a3, b3 = (r[f"{kind}3{c}"] for kind in "xsab")
        steps(
            lo3, hi3, ANY, lambda ms: down(lev2, ms, 0, 0, r["g2"], r["iw2"], s, a, x3, 2)
        )
        scaled(x3, r["w3"], s3, lo3, hi3)
        src = s3
        for turn in range(1, BOTTOM):
            dst = a3 if turn % 2 else b3
            sweep(lev3, lo3 + turn, hi3 - turn, ANY, r["g3"], [s3], [src], storing([dst]))
            src = dst
        steps(0, (N2 + 8) // 2, ANY, add(a, src, H2 - 4, H3 - 2))
        sweep(lev2, H2 - 3, H2 + N2 + 3, ANY, r["g2"], [s], [a], storing([b]))
        sweep(lev2, H2 - 2, H2 + N2 + 2, ANY, r["g2"], [s], [b], storing([a]))
        s1, a1, b1 = (r[f"{kind}1{c}"] for kind in "sab")
        steps(0, (N1 + 8) // 2, ANY, add(a1, a, H1 - 4, H2 - 2))
        sweep(lev1, 3, N1 + 2 * H1 - 3, ANY, r["g1"], [s1], [a1], storing([b1]))
        sweep(lev1, 4, N1 + 2 * H1 - 4, ANY, r["g1"], [s1], [b1], storing([a1]))

    outs = (o_0, o_1, o_2)

    def top(c):
        wide = N1 + 2
        coarse = r[f"a1{c}"][pl.ds(H1 - 1, wide)].reshape(wide * 8, LANES)
        for jh in (0, 1):
            half[c, jh] = jnp.dot(
                coarse, up_m[jh], precision=HIGHEST, preferred_element_type=F32
            ).reshape(wide, 8, LANES)
        s, a, b = r[f"s0{c}"], r[f"a0{c}"], r[f"b0{c}"]

        def refined(ms):
            for i, m in enumerate(ms):
                for jh in (0, 1):
                    for twin in (0, 1):
                        tmp[i, pl.ds(16 * jh + twin, 8, stride=2), :] = half[c, jh, m]
            made = []
            for i, m in enumerate(ms):
                for twin in (0, 1):
                    n = H0 - 2 + 2 * m + twin
                    made.append((n, b[n, BODY] + tmp[i]))
            for n, v in made:
                put(b, n, v)

        steps(0, wide, 9, refined)
        sweep(
            fine, 3, N0 + 2 * H0 - 3, 17, r["g0"], [s], [b], lambda _, n, v: put(a, n, v), BODY
        )

        def to_out(_, n, v):
            outs[c][n - H0] = v

        sweep(fine, 4, N0 + 2 * H0 - 4, 16, r["g0"], [s], [a], to_out, BODY)

    first = to_level_2(0, first)
    grid_ready(2)
    down_0(1)
    second = to_level_1(1)
    unpack(3, nu2, moving)
    steps(lo3 - 1, hi3 + 1, 12, nu_down(nu2, nu3, 0, 0, 2))
    weights(
        lev2, DIFFUSION_NUMBER / 16, lo2, hi2, 24, nu2, ALL, in2, r["g2"], r["w2"], r["iw2"]
    )
    weights(
        lev3, DIFFUSION_NUMBER / 64, lo3, hi3, ANY, nu3, ALL, in3, r["g3"], r["w3"], r["iw3"]
    )
    second = to_level_2(1, second)
    grid_ready(3)
    down_0(2)
    third = to_level_1(2)
    bottom(0, first)
    bottom(1, second)
    third = to_level_2(2, third)
    top(0)
    top(1)
    bottom(2, third)
    top(2)

    for f in range(4):
        most = mids[f].at[pl.ds(0, n_dev - 1)]
        pltpu.make_async_copy(most, most, r["send_1"].at[f]).wait()

        @pl.when((dev > 0) & (dev < n_dev - 1))
        def _():
            most = asms[f].at[pl.ds(0, n_dev - 1)]
            pltpu.make_async_copy(most, most, r["send_2"].at[f]).wait()

        @pl.when((dev == 0) | (dev == n_dev - 1))
        def _():
            most = stages[f].reshape(SIDE * SIDE // 8, 8, LANES).at[pl.ds(0, 128)]
            pltpu.make_async_copy(most, most, r["send_2"].at[f]).wait()
            rest = stages[f].reshape(SIDE * SIDE // 8, 8, LANES).at[pl.ds(0, 23)]
            pltpu.make_async_copy(rest, rest, r["send_2"].at[f]).wait()


def whole(n_dev, source, velocity_old, viscosity_old):
    vmem = pl.BlockSpec(memory_space=pltpu.VMEM)
    anywhere = pl.BlockSpec(memory_space=pltpu.HBM)
    named = names_of_scratch(n_dev)
    return pl.pallas_call(
        functools.partial(whole_kernel, tuple(named)),
        out_shape=[jax.ShapeDtypeStruct((N0, SIDE, LANES), F32)] * 3,
        in_specs=[pl.BlockSpec(memory_space=pltpu.SMEM), anywhere, anywhere],
        out_specs=[vmem] * 3,
        scratch_shapes=list(named.values()),
        compiler_params=pltpu.CompilerParams(
            collective_id=0, has_side_effects=True, vmem_limit_bytes=VMEM_LIMIT
        ),
        name="whole",
    )(source, velocity_old, viscosity_old)


def blocks_kernel(e_0, e_1, e_2, out_ref):
    for c, e in enumerate((e_0, e_1, e_2)):
        for t in range(8):
            parts = [e[pl.ds(4 * t + jj, SIDE, stride=SIDE), :] for jj in range(4)]
            turned = jnp.concatenate(parts, axis=0).T
            for at, slot in enumerate(LANE_SLOTS):
                out_ref[slot, c, :, pl.ds(t * LANES, LANES)] = turned[SIDE * at : SIDE * at + SIDE]


def to_blocks(planes):
    vmem = pl.BlockSpec(memory_space=pltpu.VMEM)
    return pl.pallas_call(
        blocks_kernel,
        out_shape=jax.ShapeDtypeStruct((4, 3, SIDE, SIDE * SIDE), F32),
        in_specs=[vmem] * 3,
        out_specs=vmem,
        compiler_params=pltpu.CompilerParams(vmem_limit_bytes=VMEM_LIMIT),
        name="to_blocks",
    )(*[p.reshape(SIDE * SIDE, LANES) for p in planes])


def solution(mesh):
    n_dev = mesh.shape["dev"]

    def local(velocity_old, viscosity_old, source):
        return to_blocks(whole(n_dev, source, velocity_old, viscosity_old))

    return jax.shard_map(
        local,
        mesh=mesh,
        in_specs=(P(("grp", "dev"), None, None, None), P(("grp", "dev"), None, None), P()),
        out_specs=P(("grp", "dev"), None, None, None),
        check_vma=False,
    )
```
